256 devices in a mesh: dp: 64 (over x, z_hi, y), vocab: 4 (over z_lo, core).
Axes of the slice: x: 4, y: 4, z: 8 (z_hi: 4, z_lo: 2; z = z_hi * 2 + z_lo), core: 2. Of those that a mesh axis runs over, the one named last changes fastest.
Arguments:
- hidden: bfloat16 [512, 4608], P('dp'), may hold values from -1.5 to 1.5
- table: bfloat16 [131072, 4608], P(('dp', 'vocab')), may hold values from -1 to 1
- target_ids: int32 [512], P('dp'), may hold values from 0 to 131071
- loss_weight: bfloat16 [512], P('dp'), may hold values from 2 to 8
- input_ids: int32 [512], P('dp'), may hold values from 0 to 131071
- emb_grad_in: bfloat16 [512, 4608], P('dp'), may hold values from -6 to 6
Outputs:
- grad_hidden: bfloat16 [512, 4608], P('dp')
- grad_table: bfloat16 [131072, 4608], P(('dp', 'vocab'))
The draws below stay inside these ranges and needn't reach their ends.
All inputs are finite; a program needn't handle non-finite values.
Results may differ from the reference program's by a relative error of at most 0.0045.
Values may be sent and summed in bfloat16 or wider, within the bound.
No kernel may reach another device: no remote copies, remote signals or barrier semaphores. Data moves between devices by JAX's collectives and lax.ppermute only.
A program may use at most 128 MiB of HBM per device.

```python
import math
import jax
import jax.numpy as jnp
import numpy as np

D = 4608
TOKENS = 512
VOC = 131072


def draw_table(key, part):
    key = jax.random.fold_in(key, 7)
    rows = jnp.arange(VOC).astype(jnp.float32)[:, None]
    scale = 16.0 / math.sqrt(D) * (1.0 + 0.07 * rows / VOC)
    base = jax.random.normal(key, (VOC, D), jnp.float32)
    return jnp.clip(base * scale, -1.0, 1.0).astype(jnp.bfloat16)


def touch_ends(entries, rng, least, top_value):
    longest = entries.shape.index(max(entries.shape))
    spots = []
    for shift in (0, 1):
        where = [jax.random.randint(jax.random.fold_in(rng, axis), (), 0, length) for axis, length in enumerate(entries.shape)]
        where[longest] = (where[longest] + shift) % entries.shape[longest]
        spots.append(tuple(where))
    return entries.at[spots[0]].set(least).at[spots[1]].set(top_value)


def levels(stream_key, shape, shards, smallest, high):
    gain = 1.0
    for dim, shards_of in shards:
        steps = jax.random.uniform(jax.random.fold_in(jax.random.fold_in(stream_key, 6), dim), (shards_of,), jnp.float32, smallest / len(shards), high / len(shards))
        gain = gain * jnp.repeat(jnp.exp(steps), shape[dim] // shards_of).reshape((-1,) + (1,) * (len(shape) - 1 - dim))
    return gain


def skewed_wide(key, dims, amount, skew):
    loads = [min(1 << octave, amount + 1 - (1 << octave)) * (1 << 20) // math.isqrt((1 << octave) ** skew) + 1 for octave in range((amount + 1).bit_length()) if 1 << octave <= amount]
    scale = 1 + sum(loads) // (1 << 30)
    table = np.cumsum(np.array([max(1, weight // scale) for weight in loads]))
    ticket = jax.random.randint(jax.random.fold_in(key, 1), dims, 0, int(table[len(loads) - 1]))
    start = jnp.left_shift(1, jnp.searchsorted(jnp.asarray(table, jnp.int32), ticket, side="right").astype(jnp.int32))
    standing = start - 1 + jax.random.randint(jax.random.fold_in(key, 4), dims, 0, 1 << 30) % jnp.minimum(start, amount + 1 - start)
    return jax.random.permutation(jax.random.fold_in(key, 2), amount)[standing].astype(jnp.int32)


def bell_draw(key, shape, width, limit, pieces=(), kind=jnp.bfloat16):
    level = levels(key, shape, pieces, -0.22, 0.18) if pieces else 1.0
    entries = jax.random.normal(key, shape, jnp.float32) * width * level
    return jnp.minimum(jnp.maximum(entries, -limit), limit).astype(kind)


def setup_inputs(seed: int = 0) -> dict:
    seeds = jax.random.split(jax.random.key(seed), 7)
    hidden = bell_draw(seeds[0], (TOKENS, D), 0.25, 1.5, ((0, 64),))
    table = draw_table(jax.random.fold_in(seeds[6], 71), 0)
    target_ids = touch_ends(jax.random.randint(seeds[2], (TOKENS,), 0, VOC), jax.random.fold_in(seeds[2], 1), 0, VOC - 1).astype(jnp.int32)
    loss_weight = jnp.clip(jnp.exp(math.log(8.0) - 1.3862944 * jax.random.uniform(seeds[3], (TOKENS,), jnp.float32) ** levels(seeds[3], (TOKENS,), ((0, 64),), -0.2, 0.2)), 2.0, 8.0).astype(jnp.bfloat16)
    input_ids = touch_ends(skewed_wide(seeds[4], (TOKENS,), VOC, 2), jax.random.fold_in(seeds[4], 3), 0, VOC - 1).astype(jnp.int32)
    emb_grad_in = bell_draw(seeds[5], (TOKENS, D), 1.0, 6.0, ((0, 64),))
    return dict(hidden=hidden, table=table, target_ids=target_ids, loss_weight=loss_weight, input_ids=input_ids, emb_grad_in=emb_grad_in)


def reference(hidden, table, target_ids, loss_weight, input_ids, emb_grad_in):
    logits = jnp.dot(hidden, table.T, preferred_element_type=jnp.float32)
    squash = jnp.tanh(logits / 30.0)
    expo = jnp.exp(30.0 * squash)
    total = jnp.sum(expo, axis=1, keepdims=True)
    columns = jnp.arange(VOC).astype(jnp.int32)
    hits = (columns[None, :] == target_ids.astype(jnp.int32)[:, None]).astype(jnp.float32)
    weight = loss_weight.astype(jnp.float32)[:, None]
    dlogit = (weight * (expo / total - hits) * (1.0 - squash * squash)).astype(jnp.bfloat16)
    grad_hidden = jnp.dot(dlogit, table, preferred_element_type=jnp.float32).astype(jnp.bfloat16)
    head = jnp.dot(dlogit.T, hidden, preferred_element_type=jnp.float32)
    embed = jax.ops.segment_sum(emb_grad_in.astype(jnp.float32), input_ids.astype(jnp.int32), num_segments=VOC)
    grad_table = (head + embed).astype(jnp.bfloat16)
    return grad_hidden, grad_table
```

```python
import jax
import jax.numpy as jnp
from jax import lax
from jax.sharding import Mesh, PartitionSpec as P

DP = ("x", "zh", "y")
AXES = ("x", "zh", "y", "zl", "c")
F32, BF16 = jnp.float32, jnp.bfloat16


def pull(value, axis, shift, size=4):
    return lax.ppermute(value, axis, [(i, (i - shift) % size) for i in range(size)])


def push(value, axis, shift, size=4):
    return lax.ppermute(value, axis, [(i, (i + shift) % size) for i in range(size)])


def swap(value, axis):
    return lax.ppermute(value, axis, [(0, 1), (1, 0)])


def digits(ids):
    return [ids // 65536, (ids // 256) % 256, ids % 256]


def joined(cols):
    return (cols[:, 0] * 65536.0 + cols[:, 1] * 256.0 + cols[:, 2]).astype(jnp.int32)


def whole(core, own, other):
    return jnp.where(
        core == 0, jnp.concatenate([own, other], 1), jnp.concatenate([other, own], 1)
    )


def body(hidden, table, target_ids, loss_weight, input_ids, emb_grad_in):
    own_rows, width = table.shape
    half = width // 2
    core = lax.axis_index("c")
    row_start = lax.axis_index(AXES) * own_rows
    tokens = hidden.shape[0] * 64
    slab = tokens // 4

    def my_half(a):
        return lax.dynamic_slice_in_dim(a, core * half, half, 1)

    def other_half(a):
        return lax.dynamic_slice_in_dim(a, (1 - core) * half, half, 1)

    emb_half = lax.all_gather(my_half(emb_grad_in), DP, axis=0, tiled=True)

    info = jnp.stack(
        [v.astype(BF16) for v in digits(target_ids) + digits(input_ids)] + [loss_weight], 1
    )
    info = jnp.pad(info, ((0, 0), (0, 128 - info.shape[1])))
    block = jnp.concatenate([my_half(hidden), info], 1)
    block = jnp.concatenate([block] + [pull(block, "zh", d) for d in (1, 2, 3)], 0)
    block = jnp.concatenate([block] + [pull(block, "y", d) for d in (1, 2, 3)], 0)
    slabs = [block] + [pull(block, "x", d) for d in (1, 2, 3)]

    pair = jnp.concatenate([my_half(table), swap(other_half(table), "c")], 0)

    facts = jnp.concatenate([s[:, half : half + 8] for s in slabs], 0).astype(F32)
    target_rel, input_rel, weight = joined(facts[:, 0:3]), joined(facts[:, 3:6]), facts[:, 6]

    place = lax.iota(jnp.int32, tokens)
    dx, dy, dz, i = place // 128, (place // 32) % 4, (place // 8) % 4, place % 8
    ax, ay, az = (lax.axis_index(n) for n in ("x", "y", "zh"))
    absolute = (((ax + dx) % 4) * 16 + ((az + dz) % 4) * 4 + (ay + dy) % 4) * 8 + i
    perm = absolute[:, None] == place[None, :]

    full, squash, expo = [], [], []
    for s in slabs:
        own = s[:, :half]
        f = whole(core, own, swap(own, "c"))
        logits = lax.dot_general(f, table, (((1,), (1,)), ((), ())), preferred_element_type=F32)
        q = jnp.tanh(logits / 30.0)
        full.append(f)
        squash.append(q)
        expo.append(jnp.exp(30.0 * q))
    squash, expo = jnp.concatenate(squash, 0), jnp.concatenate(expo, 0)
    local = jnp.sum(expo, 1)
    local = jnp.sum(jnp.where(perm, local[:, None], 0.0), 0).reshape(4, 128)
    local = lax.psum(local, "c")
    local = lax.all_to_all(jnp.broadcast_to(local, (16, 4, 128)), ("x", "y"), 0, 0)
    total = lax.psum(jnp.sum(local, 0), ("zh", "zl")).reshape(tokens)
    total = jnp.sum(jnp.where(perm, total[None, :], 0.0), 1)

    columns = row_start + lax.iota(jnp.int32, own_rows)
    hits = columns[None, :] == target_rel[:, None]
    dlogit = (
        weight[:, None]
        * (expo / total[:, None] - hits.astype(F32))
        * (1.0 - squash * squash)
    ).astype(BF16)
    both = jnp.concatenate([dlogit, swap(dlogit, "c")], 1)

    parts = [
        jnp.dot(both[d * slab : (d + 1) * slab], pair, preferred_element_type=F32)
        for d in (1, 2, 3)
    ]
    got = [push(p.astype(BF16), "x", d) for p, d in zip(parts, (1, 2, 3))]
    acc = jnp.dot(both[:slab], pair, preferred_element_type=F32)
    acc = acc + got[0].astype(F32) + got[1].astype(F32) + got[2].astype(F32)
    got = [push(acc[32 * d : 32 * d + 32].astype(BF16), "y", d) for d in (1, 2, 3)]
    acc = acc[:32] + got[0].astype(F32) + got[1].astype(F32) + got[2].astype(F32)
    got = [push(acc[8 * d : 8 * d + 8], "zh", d) for d in (1, 2, 3)]
    acc = acc[:8] + got[0] + got[1] + got[2]
    acc = (acc + swap(acc, "zl")).astype(BF16)
    grad_hidden = whole(core, acc, swap(acc, "c"))

    emb = whole(core, emb_half, swap(emb_half, "c"))
    input_abs = jnp.sum(jnp.where(perm, input_rel[:, None], 0), 0)
    onehot_in = (input_abs[:, None] == columns[None, :]).astype(BF16)
    contract = (((0,), (0,)), ((), ()))
    grad_table = lax.dot_general(
        jnp.concatenate([dlogit, onehot_in], 0),
        jnp.concatenate(full + [emb], 0),
        contract,
        preferred_element_type=F32,
    )
    return (grad_hidden, grad_table.astype(BF16))


def solution(mesh):
    fine = Mesh(mesh.devices.reshape(4, 4, 4, 2, 2), AXES)
    rows, every = P(DP, None), P(AXES, None)
    return jax.shard_map(
        body,
        mesh=fine,
        in_specs=(rows, every, P(DP), P(DP), P(DP), rows),
        out_specs=(rows, every),
        check_vma=False,
    )
```

```python
import functools

import jax
import jax.numpy as jnp
from jax import lax
from jax.experimental import pallas as pl
from jax.experimental.pallas import tpu as pltpu
from jax.sharding import Mesh, PartitionSpec as P

DP = ("x", "zh", "y")
AXES = ("x", "zh", "y", "zl", "c")
F32, BF16 = jnp.float32, jnp.bfloat16
VMEM_LIMIT = 56 * 1024 * 1024
INFO = 128
SLAB = 128
TILE = 768


def pull(value, axis, shift, size=4):
    return lax.ppermute(value, axis, [(i, (i - shift) % size) for i in range(size)])


def push(value, axis, shift, size=4):
    return lax.ppermute(value, axis, [(i, (i + shift) % size) for i in range(size)])


def swap(value, axis):
    return lax.ppermute(value, axis, [(0, 1), (1, 0)])


def digits(ids):
    return [ids // 65536, (ids // 256) % 256, ids % 256]


def info_columns(values):
    info = jnp.stack([v.astype(BF16) for v in values], 1)
    return jnp.pad(info, ((0, 0), (0, INFO - info.shape[1])))


def whole(core, own, other):
    return jnp.where(
        core == 0, jnp.concatenate([own, other], 1), jnp.concatenate([other, own], 1)
    )


def joined(info):
    info = info.astype(F32)
    return (info[:, 0:1] * 65536.0 + info[:, 1:2] * 256.0 + info[:, 2:3]).astype(jnp.int32)


def global_lane(place):
    r = lax.broadcasted_iota(jnp.int32, (SLAB, 1), 0)
    zh = (place[3] + (r // 8) % 4) % 4
    y = (place[2] + r // 32) % 4
    return zh * 32 + y * 8 + r % 8


def logits_kernel(shifts, place, *refs):
    n = len(shifts)
    own, other = refs[:n], refs[n : 2 * n]
    t_own, t_other, before, squash, expo, sums = refs[2 * n :]
    trans = (((1,), (1,)), ((), ()))

    @pl.when(pl.program_id(0) == 0)
    def _():
        sums[...] = before[...]

    acc = lax.dot_general(
        jnp.concatenate([s[...] for s in own], 0), t_own[...], trans, preferred_element_type=F32
    )
    acc += lax.dot_general(
        jnp.concatenate([s[...] for s in other], 0), t_other[...], trans, preferred_element_type=F32
    )
    q = jnp.tanh(acc * (1.0 / 30.0))
    e = jnp.exp(30.0 * q)
    squash[...] = q
    expo[...] = e
    lanes = lax.broadcasted_iota(jnp.int32, (SLAB, SLAB), 1)
    hit = lanes == global_lane(place)
    rows = lax.broadcasted_iota(jnp.int32, (4, SLAB), 0)
    add = jnp.zeros((4, SLAB), F32)
    for k, shift in enumerate(shifts):
        row = jnp.sum(e[k * SLAB : (k + 1) * SLAB], 1, keepdims=True)
        lane = jnp.sum(jnp.where(hit, row, 0.0), 0, keepdims=True)
        add = add + jnp.where(rows == (place[1] + shift) % 4, lane, 0.0)
    sums[...] += add


def logits_call(place, shifts, own, other, table, before):
    n, (rows, width) = len(shifts), table.shape
    half, tile = width // 2, rows // 2
    slab_spec = pl.BlockSpec((SLAB, half), lambda v, p: (0, 0))
    out = pl.BlockSpec((n * SLAB, tile), lambda v, p: (0, v))
    small = pl.BlockSpec((4, SLAB), lambda v, p: (0, 0))
    return pl.pallas_call(
        functools.partial(logits_kernel, shifts),
        grid_spec=pltpu.PrefetchScalarGridSpec(
            num_scalar_prefetch=1,
            grid=(rows // tile,),
            in_specs=[slab_spec] * (2 * n)
            + [
                pl.BlockSpec((tile, half), lambda v, p: (v, p[0])),
                pl.BlockSpec((tile, half), lambda v, p: (v, 1 - p[0])),
                small,
            ],
            out_specs=[out, out, small],
        ),
        out_shape=[
            jax.ShapeDtypeStruct((n * SLAB, rows), F32),
            jax.ShapeDtypeStruct((n * SLAB, rows), F32),
            jax.ShapeDtypeStruct((4, SLAB), F32),
        ],
        compiler_params=pltpu.CompilerParams(vmem_limit_bytes=VMEM_LIMIT),
    )(place, *own, *other, table, table, before)


def dlogit_kernel(place, i0, i1, i2, i3, q0, q1, e0, e1, total, out):
    hit_lane = lax.broadcasted_iota(jnp.int32, (SLAB, SLAB), 1) == global_lane(place)
    columns = place[4] + lax.broadcasted_iota(jnp.int32, (SLAB, out.shape[1]), 1)
    for d, info in enumerate((i0, i1, i2, i3)):
        q, e = (q0, e0) if d == 0 else (q1, e1)
        part = pl.ds(max(d - 1, 0) * SLAB, SLAB)
        tot = jnp.zeros((1, SLAB), F32)
        for k in range(4):
            tot = jnp.where((place[1] + d) % 4 == k, total[k : k + 1, :], tot)
        tot = jnp.sum(jnp.where(hit_lane, tot, 0.0), 1, keepdims=True)
        hits = (columns == joined(info[...])).astype(F32)
        weight = info[:, 3:4].astype(F32)
        s = q[part, :]
        out[pl.ds(d * SLAB, SLAB), :] = (
            weight * (e[part, :] / tot - hits) * (1.0 - s * s)
        ).astype(BF16)


def dlogit_call(place, slabs, q, e, total):
    rows, half = q[0].shape[1], slabs[0].shape[1] - INFO
    every = lambda a: pl.BlockSpec(a.shape, lambda i, p: (0, 0))
    return pl.pallas_call(
        dlogit_kernel,
        grid_spec=pltpu.PrefetchScalarGridSpec(
            num_scalar_prefetch=1,
            grid=(1,),
            in_specs=[pl.BlockSpec((SLAB, INFO), lambda i, p: (0, half // INFO))] * 4
            + [every(a) for a in (*q, *e, total)],
            out_specs=pl.BlockSpec((4 * SLAB, rows), lambda i, p: (0, 0)),
        ),
        out_shape=jax.ShapeDtypeStruct((4 * SLAB, rows), BF16),
        compiler_params=pltpu.CompilerParams(vmem_limit_bytes=VMEM_LIMIT),
    )(place, *slabs, *q, *e, total)


def hidden_grad_kernel(place, own, other, t_own, t_other, g0, g1, g2, g3):
    acc = jnp.dot(own[...], t_own[...], preferred_element_type=F32)
    acc += jnp.dot(other[...], t_other[...], preferred_element_type=F32)
    for d, g in enumerate((g0, g1, g2, g3)):
        g[...] = acc[d * SLAB : (d + 1) * SLAB].astype(g.dtype)


def hidden_grad_call(place, own, other, table, t_other):
    rows, half = t_other.shape
    steps = half // TILE
    full = pl.BlockSpec(own.shape, lambda j, p: (0, 0))
    return pl.pallas_call(
        hidden_grad_kernel,
        grid_spec=pltpu.PrefetchScalarGridSpec(
            num_scalar_prefetch=1,
            grid=(steps,),
            in_specs=[
                full,
                full,
                pl.BlockSpec((rows, TILE), lambda j, p: (0, p[0] * steps + j)),
                pl.BlockSpec((rows, TILE), lambda j, p: (0, j)),
            ],
            out_specs=[pl.BlockSpec((SLAB, TILE), lambda j, p: (0, j))] * 4,
        ),
        out_shape=[jax.ShapeDtypeStruct((SLAB, half), F32)]
        + [jax.ShapeDtypeStruct((SLAB, half), BF16)] * 3,
        compiler_params=pltpu.CompilerParams(vmem_limit_bytes=VMEM_LIMIT),
    )(place, own, other, table, t_other)


def table_grad_kernel(place, dlogit, i0, i1, i2, i3, *refs):
    blocks, out, turned = refs[:16], refs[16], refs[17]
    h, j = pl.program_id(0), pl.program_id(1)
    tokens, rows = dlogit.shape

    @pl.when((h == 0) & (j == 0))
    def _():
        turned[:, :tokens] = dlogit[...].T
        columns = place[4] + lax.broadcasted_iota(jnp.int32, (SLAB, rows), 1)
        for d, info in enumerate((i0, i1, i2, i3)):
            hit = (columns == joined(info[...])).astype(F32).astype(BF16)
            turned[:, tokens + d * SLAB : tokens + (d + 1) * SLAB] = hit.T

    def product(group):
        right = jnp.concatenate([r[...] for r in group], 0)
        out[...] = jnp.dot(turned[...], right, preferred_element_type=F32).astype(BF16)

    @pl.when(h == 0)
    def _():
        product(blocks[:8])

    @pl.when(h == 1)
    def _():
        product(blocks[8:])


def table_grad_call(place, dlogit, own, other):
    tokens, rows = dlogit.shape
    half = own[0].shape[1] - INFO
    steps = half // TILE
    first = pl.BlockSpec((SLAB, TILE), lambda h, j, p: (0, jnp.where(h == 0, j, steps - 1)))
    second = pl.BlockSpec((SLAB, TILE), lambda h, j, p: (0, jnp.where(h == 1, j, 0)))
    return pl.pallas_call(
        table_grad_kernel,
        grid_spec=pltpu.PrefetchScalarGridSpec(
            num_scalar_prefetch=1,
            grid=(2, steps),
            in_specs=[pl.BlockSpec((tokens, rows), lambda h, j, p: (0, 0))]
            + [pl.BlockSpec((SLAB, INFO), lambda h, j, p: (0, half // INFO))] * 4
            + [first] * 8
            + [second] * 8,
            out_specs=pl.BlockSpec(
                (rows, TILE),
                lambda h, j, p: (0, jnp.where(h == 0, p[0], 1 - p[0]) * steps + j),
            ),
            scratch_shapes=[pltpu.VMEM((rows, 2 * tokens), BF16)],
        ),
        out_shape=jax.ShapeDtypeStruct((rows, 2 * half), BF16),
        compiler_params=pltpu.CompilerParams(vmem_limit_bytes=VMEM_LIMIT),
    )(place, dlogit, *own[4:], *own, *other)


def body(hidden, table, target_ids, loss_weight, input_ids, emb_grad_in):
    own_rows, width = table.shape
    half = width // 2
    core = lax.axis_index("c")
    row_start = lax.axis_index(AXES) * own_rows
    place = jnp.stack(
        [core, lax.axis_index("x"), lax.axis_index("y"), lax.axis_index("zh"), row_start]
    ).astype(jnp.int32)

    def my_half(a):
        return lax.dynamic_slice_in_dim(a, core * half, half, 1)

    joint = jnp.concatenate(
        [
            my_half(hidden),
            info_columns(digits(target_ids) + [loss_weight]),
            my_half(emb_grad_in),
            info_columns(digits(input_ids)),
        ],
        1,
    )
    joint = [joint] + [pull(joint, "zh", d) for d in (1, 2, 3)]
    hid = jnp.concatenate([b[:, : half + INFO] for b in joint], 0)
    emb = jnp.concatenate([b[:, half + INFO :] for b in joint], 0)
    hid = jnp.concatenate([hid] + [pull(hid, "y", d) for d in (1, 2, 3)], 0)
    hids = [hid] + [pull(hid, "x", d) for d in (1, 2, 3)]
    emb = jnp.concatenate([emb] + [pull(emb, "x", d) for d in (1, 2, 3)], 0)
    embs = [emb] + [pull(emb, "y", d) for d in (1, 2, 3)]
    t_other = swap(lax.dynamic_slice_in_dim(table, (1 - core) * half, half, 1), "c")

    others = [swap(s, "c") for s in hids]
    q0, e0, sums = logits_call(
        place, (0,), hids[:1], others[:1], table, jnp.zeros((4, SLAB), F32)
    )
    q1, e1, sums = logits_call(place, (1, 2, 3), hids[1:], others[1:], table, sums)
    total = sums
    for axes in (("zh", "zl", "c"), ("x", "y")):
        total = jnp.sum(
            lax.all_to_all(jnp.broadcast_to(total, (16, 4, SLAB)), axes, 0, 0), 0
        )

    dlogit = dlogit_call(place, hids, (q0, q1), (e0, e1), total)
    acc, *parts = hidden_grad_call(place, dlogit, swap(dlogit, "c"), table, t_other)
    got = [push(p, "x", d) for p, d in zip(parts, (1, 2, 3))]
    acc = acc + got[0].astype(F32) + got[1].astype(F32) + got[2].astype(F32)
    got = [push(acc[32 * d : 32 * d + 32].astype(BF16), "y", d) for d in (1, 2, 3)]
    acc = acc[:32] + got[0].astype(F32) + got[1].astype(F32) + got[2].astype(F32)
    got = [push(acc[8 * d : 8 * d + 8], "zh", d) for d in (1, 2, 3)]
    acc = acc[:8] + got[0] + got[1] + got[2]
    acc = (acc + swap(acc, "zl")).astype(BF16)
    grad_hidden = whole(core, acc, swap(acc, "c"))

    emb_others = [swap(s, "c") for s in embs]
    grad_table = table_grad_call(place, dlogit, hids + embs, others + emb_others)
    return grad_hidden, grad_table


def solution(mesh):
    fine = Mesh(mesh.devices.reshape(4, 4, 4, 2, 2), AXES)
    rows, every = P(DP, None), P(AXES, None)
    return jax.shard_map(
        body,
        mesh=fine,
        in_specs=(rows, every, P(DP), P(DP), P(DP), rows),
        out_specs=(rows, every),
        check_vma=False,
    )
```

```python
import functools

import jax
import jax.numpy as jnp
from jax import lax
from jax.experimental import pallas as pl
from jax.experimental.pallas import tpu as pltpu
from jax.sharding import Mesh, PartitionSpec as P

DP = ("x", "zh", "y")
AXES = ("x", "zh", "y", "zl", "c")
F32, BF16 = jnp.float32, jnp.bfloat16
VMEM_LIMIT = 56 * 1024 * 1024
INFO = 128
SLAB = 128
TILE = 768


def pull(value, axis, shift, size=4):
    return lax.ppermute(value, axis, [(i, (i - shift) % size) for i in range(size)])


def push(value, axis, shift, size=4):
    return lax.ppermute(value, axis, [(i, (i + shift) % size) for i in range(size)])


def swap(value, axis):
    return lax.ppermute(value, axis, [(0, 1), (1, 0)])


def digits(ids):
    return [ids // 65536, (ids // 256) % 256, ids % 256]


def info_columns(values):
    info = jnp.stack([v.astype(BF16) for v in values], 1)
    return jnp.pad(info, ((0, 0), (0, INFO - info.shape[1])))


def whole(core, own, other):
    return jnp.where(
        core == 0, jnp.concatenate([own, other], 1), jnp.concatenate([other, own], 1)
    )


def joined(info):
    info = info.astype(F32)
    return (info[:, 0:1] * 65536.0 + info[:, 1:2] * 256.0 + info[:, 2:3]).astype(jnp.int32)


def global_lane(place):
    r = lax.broadcasted_iota(jnp.int32, (SLAB, 1), 0)
    zh = (place[3] + (r // 8) % 4) % 4
    y = (place[2] + r // 32) % 4
    return zh * 32 + y * 8 + r % 8


def logits_kernel(shifts, place, *refs):
    n = len(shifts)
    own, other, infos = refs[:n], refs[n : 2 * n], refs[2 * n : 3 * n]
    t_own, t_other, before, squash, expo, slope, sums = refs[3 * n :]
    trans = (((1,), (1,)), ((), ()))
    step, tile = pl.program_id(0), expo.shape[1]

    @pl.when(step == 0)
    def _():
        sums[...] = before[...]

    acc = lax.dot_general(
        jnp.concatenate([s[...] for s in own], 0), t_own[...], trans, preferred_element_type=F32
    )
    acc += lax.dot_general(
        jnp.concatenate([s[...] for s in other], 0), t_other[...], trans, preferred_element_type=F32
    )
    q = jnp.tanh(acc * (1.0 / 30.0))
    e = jnp.exp(30.0 * q)
    squash[...] = q
    expo[...] = e
    columns = place[4] + step * tile + lax.broadcasted_iota(jnp.int32, (SLAB, tile), 1)
    hit_lane = lax.broadcasted_iota(jnp.int32, (SLAB, SLAB), 1) == global_lane(place)
    rows = lax.broadcasted_iota(jnp.int32, (8, SLAB), 0)
    add = jnp.zeros((8, SLAB), F32)
    for k, shift in enumerate(shifts):
        part = slice(k * SLAB, (k + 1) * SLAB)
        hits = columns == joined(infos[k][...])
        qk, ek = q[part], e[part]
        slope[part, :] = jnp.where(hits, 0.0, ek * (1.0 - qk * qk)).astype(BF16)
        at = (place[1] + shift) % 4
        for base, values in ((0, ek), (4, jnp.where(hits, qk, 0.0))):
            row = jnp.sum(values, 1, keepdims=True)
            lane = jnp.sum(jnp.where(hit_lane, row, 0.0), 0, keepdims=True)
            add = add + jnp.where(rows == at + base, lane, 0.0)
    sums[...] += add


def logits_call(place, shifts, own, other, table, before):
    n, (rows, width) = len(shifts), table.shape
    half, tile = width // 2, rows // 2
    slab_spec = pl.BlockSpec((SLAB, half), lambda v, p: (0, 0))
    out = pl.BlockSpec((n * SLAB, tile), lambda v, p: (0, v))
    small = pl.BlockSpec((8, SLAB), lambda v, p: (0, 0))
    return pl.pallas_call(
        functools.partial(logits_kernel, shifts),
        grid_spec=pltpu.PrefetchScalarGridSpec(
            num_scalar_prefetch=1,
            grid=(rows // tile,),
            in_specs=[slab_spec] * (2 * n)
            + [pl.BlockSpec((SLAB, INFO), lambda v, p: (0, half // INFO))] * n
            + [
                pl.BlockSpec((tile, half), lambda v, p: (v, p[0])),
                pl.BlockSpec((tile, half), lambda v, p: (v, 1 - p[0])),
                small,
            ],
            out_specs=[out, out, out, small],
        ),
        out_shape=[
            jax.ShapeDtypeStruct((n * SLAB, rows), F32),
            jax.ShapeDtypeStruct((n * SLAB, rows), F32),
            jax.ShapeDtypeStruct((n * SLAB, rows), BF16),
            jax.ShapeDtypeStruct((8, SLAB), F32),
        ],
        compiler_params=pltpu.CompilerParams(vmem_limit_bytes=VMEM_LIMIT),
        cost_estimate=cost(n * SLAB * rows * width),
        name="logits",
    )(place, *own, *other, *own, table, table, before)


def cost(macs):
    return pl.CostEstimate(flops=4 * macs, bytes_accessed=10_000_000, transcendentals=0)


def dlogit_kernel(place, *refs):
    infos, embs = refs[:4], refs[4:8]
    q0, q1, e0, e1, total, turned = refs[8:]
    hit_lane = lax.broadcasted_iota(jnp.int32, (SLAB, SLAB), 1) == global_lane(place)
    columns = place[4] + lax.broadcasted_iota(jnp.int32, (SLAB, turned.shape[0]), 1)
    for d in range(4):
        q, e = (q0, e0) if d == 0 else (q1, e1)
        part = pl.ds(max(d - 1, 0) * SLAB, SLAB)
        tot = jnp.zeros((1, SLAB), F32)
        for k in range(4):
            tot = jnp.where((place[1] + d) % 4 == k, total[k : k + 1, :], tot)
        tot = jnp.sum(jnp.where(hit_lane, tot, 0.0), 1, keepdims=True)
        hits = (columns == joined(infos[d][...])).astype(F32)
        weight = infos[d][:, 3:4].astype(F32)
        s = q[part, :]
        value = (weight * (e[part, :] / tot - hits) * (1.0 - s * s)).astype(BF16)
        turned[:, d * SLAB : (d + 1) * SLAB] = value.T
        hit = (columns == joined(embs[d][...])).astype(F32).astype(BF16)
        turned[:, (4 + d) * SLAB : (5 + d) * SLAB] = hit.T


def dlogit_call(place, slabs, embs, q, e, total):
    rows, half = q[0].shape[1], slabs[0].shape[1] - INFO
    every = lambda a: pl.BlockSpec(a.shape, lambda i, p: (0, 0))
    return pl.pallas_call(
        dlogit_kernel,
        grid_spec=pltpu.PrefetchScalarGridSpec(
            num_scalar_prefetch=1,
            grid=(1,),
            in_specs=[pl.BlockSpec((SLAB, INFO), lambda i, p: (0, half // INFO))] * 8
            + [every(a) for a in (*q, *e, total)],
            out_specs=pl.BlockSpec((rows, 8 * SLAB), lambda i, p: (0, 0)),
        ),
        out_shape=jax.ShapeDtypeStruct((rows, 8 * SLAB), BF16),
        compiler_params=pltpu.CompilerParams(vmem_limit_bytes=VMEM_LIMIT),
        cost_estimate=cost(1 << 29),
        name="dlogit",
    )(place, *slabs, *embs, *q, *e, total)


def slope_product_kernel(place, own, other, t_own, t_other, *outs):
    acc = jnp.dot(own[...], t_own[...], preferred_element_type=F32)
    acc += jnp.dot(other[...], t_other[...], preferred_element_type=F32)
    for d, g in enumerate(outs):
        g[...] = acc[d * SLAB : (d + 1) * SLAB].astype(g.dtype)


def pick_kernel(place, info, t_own, t_other, *refs):
    outs, mine, theirs = refs[:4], refs[4], refs[5]

    @pl.when(pl.program_id(0) == 0)
    def _():
        ids = joined(info[...])
        columns = lax.broadcasted_iota(jnp.int32, mine.shape, 1)
        mine[...] = (columns + place[4] == ids).astype(F32).astype(BF16)
        theirs[...] = (columns + place[5] == ids).astype(F32).astype(BF16)

    acc = jnp.dot(mine[...], t_own[...], preferred_element_type=F32)
    acc += jnp.dot(theirs[...], t_other[...], preferred_element_type=F32)
    for d, g in enumerate(outs):
        g[...] = acc[d * SLAB : (d + 1) * SLAB].astype(g.dtype)


def table_product(kernel, place, left, table, t_other, outs, scratch, name):
    rows, half = t_other.shape
    steps = half // TILE
    return pl.pallas_call(
        kernel,
        grid_spec=pltpu.PrefetchScalarGridSpec(
            num_scalar_prefetch=1,
            grid=(steps,),
            in_specs=[pl.BlockSpec(a.shape, lambda j, p: (0, 0)) for a in left]
            + [
                pl.BlockSpec((rows, TILE), lambda j, p: (0, p[0] * steps + j)),
                pl.BlockSpec((rows, TILE), lambda j, p: (0, j)),
            ],
            out_specs=[pl.BlockSpec((SLAB, TILE), lambda j, p: (0, j))] * len(outs),
            scratch_shapes=scratch,
        ),
        out_shape=[jax.ShapeDtypeStruct((SLAB, half), t) for t in outs],
        compiler_params=pltpu.CompilerParams(vmem_limit_bytes=VMEM_LIMIT),
        cost_estimate=cost(len(outs) * SLAB * 2 * rows * half),
        name=name,
    )(place, *left, table, t_other)


def table_grad_kernel(place, turned, *refs):
    blocks, out = refs[:8], refs[-1]
    right = jnp.concatenate([r[...] for r in blocks], 0)
    out[...] = jnp.dot(turned[...], right, preferred_element_type=F32).astype(BF16)


def table_grad_call(place, turned, slabs, other, before=None):
    rows, half = turned.shape[0], slabs[0].shape[1] - INFO
    steps = half // TILE
    return pl.pallas_call(
        table_grad_kernel,
        grid_spec=pltpu.PrefetchScalarGridSpec(
            num_scalar_prefetch=1,
            grid=(steps,),
            in_specs=[pl.BlockSpec(turned.shape, lambda j, p: (0, 0))]
            + [pl.BlockSpec((SLAB, TILE), lambda j, p: (0, j))] * 8
            + ([] if before is None else [pl.BlockSpec(memory_space=pl.ANY)]),
            out_specs=pl.BlockSpec(
                (rows, TILE),
                lambda j, p: (0, (1 - p[0] if other else p[0]) * steps + j),
            ),
        ),
        out_shape=jax.ShapeDtypeStruct((rows, 2 * half), BF16),
        input_output_aliases={} if before is None else {10: 0},
        compiler_params=pltpu.CompilerParams(vmem_limit_bytes=VMEM_LIMIT),
        cost_estimate=cost(rows * 8 * SLAB * half),
        name="table_grad",
    )(place, turned, *slabs, *([] if before is None else [before]))


def body(hidden, table, target_ids, loss_weight, input_ids, emb_grad_in):
    own_rows, width = table.shape
    half = width // 2
    core, ax, ay, az = (lax.axis_index(n) for n in ("c", "x", "y", "zh"))
    row_start = lax.axis_index(AXES) * own_rows
    place = jnp.stack(
        [core, ax, ay, az, row_start, row_start + (1 - 2 * core) * own_rows]
    ).astype(jnp.int32)

    def my_half(a):
        return lax.dynamic_slice_in_dim(a, core * half, half, 1)

    joint = jnp.concatenate(
        [
            my_half(hidden),
            info_columns(digits(target_ids) + [loss_weight]),
            my_half(emb_grad_in),
            info_columns(digits(input_ids)),
        ],
        1,
    )
    joint = [joint] + [pull(joint, "zh", d) for d in (1, 2, 3)]
    hid = jnp.concatenate([b[:, : half + INFO] for b in joint], 0)
    emb = jnp.concatenate([b[:, half + INFO :] for b in joint], 0)
    hid = [hid] + [pull(hid, "y", d) for d in (1, 2, 3)]
    emb = [emb] + [pull(emb, "x", d) for d in (1, 2, 3)]
    t_other = swap(lax.dynamic_slice_in_dim(table, (1 - core) * half, half, 1), "c")
    hid, emb, t_other = lax.optimization_barrier((hid, emb, t_other))
    hid, emb = jnp.concatenate(hid, 0), jnp.concatenate(emb, 0)
    hids = [pull(hid, "x", d) for d in (1, 2, 3)]
    embs = [pull(emb, "y", d) for d in (1, 2, 3)]

    hid_other = swap(hid, "c")
    q0, e0, slope0, sums = logits_call(
        place, (0,), [hid], [hid_other], table, jnp.zeros((8, SLAB), F32)
    )
    hids, embs, sums = lax.optimization_barrier((hids, embs, sums))
    others = [swap(s, "c") for s in hids]
    q1, e1, slope1, sums = logits_call(place, (1, 2, 3), hids, others, table, sums)
    hids, embs, others = [hid] + hids, [emb] + embs, [hid_other] + others

    parts = table_product(
        slope_product_kernel, place, [slope1, swap(slope1, "c")], table, t_other,
        [BF16] * 3, [], "slope_product",
    )
    got = [push(p, "x", d) for p, d in zip(parts, (1, 2, 3))]
    info = jnp.concatenate([s[:, half:].reshape(4, 32, INFO) for s in hids], 1)
    pick, *parts = table_product(
        pick_kernel, place, [info.reshape(4 * SLAB, INFO)], table, t_other,
        [BF16] * 4, [pltpu.VMEM((4 * SLAB, own_rows), BF16)] * 2, "pick",
    )
    got_pick = [push(p, "y", d) for p, d in zip(parts, (1, 2, 3))]
    (mean,) = table_product(
        slope_product_kernel, place, [slope0, swap(slope0, "c")], table, t_other,
        [F32], [], "slope_product",
    )

    total = sums
    for axes in (("zh", "zl", "c"), ("x", "y")):
        total = jnp.sum(
            lax.all_to_all(jnp.broadcast_to(total, (16, 8, SLAB)), axes, 0, 0), 0
        )

    mean = mean + got[0].astype(F32) + got[1].astype(F32) + got[2].astype(F32)
    pick = pick + got_pick[0] + got_pick[1] + got_pick[2]
    got = [push(mean[32 * d : 32 * d + 32].astype(BF16), "y", d) for d in (1, 2, 3)]
    got_pick = [push(pick[32 * d : 32 * d + 32], "x", d) for d in (1, 2, 3)]
    mean = mean[:32] + got[0].astype(F32) + got[1].astype(F32) + got[2].astype(F32)
    pick = pick[:32] + got_pick[0] + got_pick[1] + got_pick[2]
    both = jnp.concatenate([mean.astype(BF16), pick], 1)
    got = [push(both[8 * d : 8 * d + 8], "zh", d).astype(F32) for d in (1, 2, 3)]
    mean = mean[:8] + got[0][:, :half] + got[1][:, :half] + got[2][:, :half]
    pick = pick[:8].astype(F32) + got[0][:, half:] + got[1][:, half:] + got[2][:, half:]

    flat = total.reshape(8 * SLAB)
    start = (ax * 16 + az * 4 + ay) * 8
    norm = lax.dynamic_slice_in_dim(flat, start, 8, 0)
    s = lax.dynamic_slice_in_dim(flat, 4 * SLAB + start, 8, 0)
    weight = loss_weight.astype(F32)
    at_target = weight * (jnp.exp(30.0 * s) / norm - 1.0) * (1.0 - s * s)
    acc = mean * (weight / norm)[:, None] + pick * at_target[:, None]
    acc = (acc + swap(acc, "zl")).astype(BF16)
    grad_hidden = whole(core, acc, swap(acc, "c"))

    turned = dlogit_call(place, hids, embs, (q0, q1), (e0, e1), total)
    emb_others = [swap(s, "c") for s in embs]
    grad_table = table_grad_call(place, turned, hids + embs, 0)
    grad_table = table_grad_call(place, turned, others + emb_others, 1, grad_table)
    return grad_hidden, grad_table


def solution(mesh):
    fine = Mesh(mesh.devices.reshape(4, 4, 4, 2, 2), AXES)
    rows, every = P(DP, None), P(AXES, None)
    return jax.shard_map(
        body,
        mesh=fine,
        in_specs=(rows, every, P(DP), P(DP), P(DP), rows),
        out_specs=(rows, every),
        check_vma=False,
    )
```

```python
import functools

import jax
import jax.numpy as jnp
from jax import lax
from jax.experimental import pallas as pl
from jax.experimental.pallas import tpu as pltpu
from jax.sharding import Mesh, PartitionSpec as P

DP = ("x", "zh", "y")
AXES = ("x", "zh", "y", "zl", "c")
F32, BF16 = jnp.float32, jnp.bfloat16
VMEM_LIMIT = 56 * 1024 * 1024
INFO = 128
SLAB = 128
TILE = 1152
PRODUCTS = 10_000


def pull(value, axis, shift, size=4):
    return lax.ppermute(value, axis, [(i, (i - shift) % size) for i in range(size)])


def push(value, axis, shift, size=4):
    return lax.ppermute(value, axis, [(i, (i + shift) % size) for i in range(size)])


def swap(value, axis):
    return lax.ppermute(value, axis, [(0, 1), (1, 0)])


def digits(ids):
    return [ids // 65536, (ids // 256) % 256, ids % 256]


def info_columns(values):
    info = jnp.stack([v.astype(BF16) for v in values], 1)
    return jnp.pad(info, ((0, 0), (0, INFO - info.shape[1])))


def whole(core, own, other):
    return jnp.where(
        core == 0, jnp.concatenate([own, other], 1), jnp.concatenate([other, own], 1)
    )


def joined(info):
    info = info.astype(F32)
    return (info[:, 0:1] * 65536.0 + info[:, 1:2] * 256.0 + info[:, 2:3]).astype(jnp.int32)


def cost(us):
    return pl.CostEstimate(flops=us * 1_000_000_000 + 1, bytes_accessed=1, transcendentals=0)


def params():
    return pltpu.CompilerParams(vmem_limit_bytes=VMEM_LIMIT)


def matching(place):
    r = lax.broadcasted_iota(jnp.int32, (SLAB, SLAB), 0)
    lane = lax.broadcasted_iota(jnp.int32, (SLAB, SLAB), 1)
    zh = (place[1] + (r // 8) % 4) % 4
    return lane == (r // 32) * 32 + zh * 8 + r % 8


def as_lanes(match, column):
    return jnp.sum(jnp.where(match, column, 0.0), 0, keepdims=True)


def as_column(match, lanes):
    return jnp.sum(jnp.where(match, lanes, 0.0), 1, keepdims=True)


def logits_kernel(place, own, other, info, t_own, t_other, _, squash, expo, slope, sums):
    trans = (((1,), (1,)), ((), ()))
    step, tile = pl.program_id(0), expo.shape[1]

    @pl.when(step == 0)
    def _():
        sums[...] = jnp.zeros_like(sums)

    acc = lax.dot_general(own[...], t_own[...], trans, preferred_element_type=F32)
    acc += lax.dot_general(other[...], t_other[...], trans, preferred_element_type=F32)
    q = jnp.tanh(acc * (1.0 / 30.0))
    e = jnp.exp(30.0 * q)
    squash[...] = q
    expo[...] = e
    columns = place[2] + step * tile + lax.broadcasted_iota(jnp.int32, (SLAB, tile), 1)
    rows = lax.broadcasted_iota(jnp.int32, (8, SLAB), 0)
    match = matching(place)
    add = jnp.zeros((8, SLAB), F32)
    for d in range(4):
        part = slice(d * SLAB, (d + 1) * SLAB)
        hits = columns == joined(info[part, :])
        qd, ed = q[part], e[part]
        slope[part, :] = jnp.where(hits, 0.0, ed * (1.0 - qd * qd)).astype(BF16)
        for base, values in ((0, ed), (4, jnp.where(hits, qd, 0.0))):
            lanes = as_lanes(match, jnp.sum(values, 1, keepdims=True))
            add = add + jnp.where(rows == d + base, lanes, 0.0)
    sums[...] += add


def logits_call(place, own, other, table, after):
    (rows, width), tokens = table.shape, own.shape[0]
    half, tile = width // 2, rows // 2
    whole_block = pl.BlockSpec((tokens, half), lambda v, p: (0, 0))
    out = pl.BlockSpec((tokens, tile), lambda v, p: (0, v))
    return pl.pallas_call(
        logits_kernel,
        grid_spec=pltpu.PrefetchScalarGridSpec(
            num_scalar_prefetch=1,
            grid=(rows // tile,),
            in_specs=[
                whole_block,
                whole_block,
                pl.BlockSpec((tokens, INFO), lambda v, p: (0, half // INFO)),
                pl.BlockSpec((tile, half), lambda v, p: (v, p[0])),
                pl.BlockSpec((tile, half), lambda v, p: (v, 1 - p[0])),
                pl.BlockSpec(memory_space=pl.ANY),
            ],
            out_specs=[out, out, out, pl.BlockSpec((8, SLAB), lambda v, p: (0, 0))],
        ),
        out_shape=[
            jax.ShapeDtypeStruct((tokens, rows), F32),
            jax.ShapeDtypeStruct((tokens, rows), F32),
            jax.ShapeDtypeStruct((tokens, rows), BF16),
            jax.ShapeDtypeStruct((8, SLAB), F32),
        ],
        compiler_params=params(),
        cost_estimate=cost(PRODUCTS),
        name="logits",
    )(place, own, other, own, table, table, after)


def mean_kernel(place, own, other, t_own, t_other, out):
    acc = jnp.dot(own[...], t_own[...], preferred_element_type=F32)
    out[...] = acc + jnp.dot(other[...], t_other[...], preferred_element_type=F32)


def pick_kernel(place, info, _, t_own, t_other, out, mine, theirs):
    @pl.when(pl.program_id(0) == 0)
    def _():
        columns = lax.broadcasted_iota(jnp.int32, mine.shape, 1)
        ids = joined(info[...])
        mine[...] = (columns + place[2] == ids).astype(F32).astype(BF16)
        theirs[...] = (columns + place[3] == ids).astype(F32).astype(BF16)

    acc = jnp.dot(mine[...], t_own[...], preferred_element_type=F32)
    acc += jnp.dot(theirs[...], t_other[...], preferred_element_type=F32)
    out[...] = acc.astype(BF16)


def product_call(kernel, place, left, specs, table, t_other, kind, scratch, name):
    (rows, half), tokens = t_other.shape, 4 * SLAB
    steps = half // TILE
    return pl.pallas_call(
        kernel,
        grid_spec=pltpu.PrefetchScalarGridSpec(
            num_scalar_prefetch=1,
            grid=(steps,),
            in_specs=specs
            + [
                pl.BlockSpec((rows, TILE), lambda j, p: (0, p[0] * steps + j)),
                pl.BlockSpec((rows, TILE), lambda j, p: (0, j)),
            ],
            out_specs=pl.BlockSpec((tokens, TILE), lambda j, p: (0, j)),
            scratch_shapes=scratch,
        ),
        out_shape=jax.ShapeDtypeStruct((tokens, half), kind),
        compiler_params=params(),
        cost_estimate=cost(PRODUCTS),
        name=name,
    )(place, *left, table, t_other)


def total_kernel(got, _, out):
    acc = got[0]
    for k in range(1, got.shape[0]):
        acc += got[k]
    out[...] = acc


def total_call(value, axes, after):
    got = spread(value, axes)
    return pl.pallas_call(
        total_kernel,
        in_specs=[pl.BlockSpec(memory_space=pltpu.VMEM), pl.BlockSpec(memory_space=pl.ANY)],
        out_specs=pl.BlockSpec(memory_space=pltpu.VMEM),
        out_shape=jax.ShapeDtypeStruct(value.shape, value.dtype),
        compiler_params=params(),
        cost_estimate=cost(0),
        name="total",
    )(got, after)


def combine_kernel(place, info, mean, pick, total, out):
    match = matching(place)
    for d in range(4):
        part = pl.ds(d * SLAB, SLAB)
        norm = as_column(match, total[d : d + 1, :])
        s = as_column(match, total[d + 4 : d + 5, :])
        weight = info[part, 3:4].astype(F32)
        target = weight * (jnp.exp(30.0 * s) / norm - 1.0) * (1.0 - s * s)
        value = mean[part, :] * (weight / norm) + pick[part, :].astype(F32) * target
        out[part, :] = value.astype(BF16)


def combine_call(place, hid, mean, pick, total):
    tokens, half = mean.shape
    block = pl.BlockSpec((tokens, TILE), lambda j, p: (0, j))
    return pl.pallas_call(
        combine_kernel,
        grid_spec=pltpu.PrefetchScalarGridSpec(
            num_scalar_prefetch=1,
            grid=(half // TILE,),
            in_specs=[pl.BlockSpec((tokens, INFO), lambda j, p: (0, half // INFO))]
            + [block, block, pl.BlockSpec((8, SLAB), lambda j, p: (0, 0))],
            out_specs=block,
        ),
        out_shape=jax.ShapeDtypeStruct((tokens, half), BF16),
        compiler_params=params(),
        cost_estimate=cost(0),
        name="combine",
    )(place, hid, mean, pick, total)


def sum_kernel(got, _, out):
    acc = got[0].astype(F32)
    for k in range(1, got.shape[0]):
        acc += got[k].astype(F32)
    out[...] = acc.astype(BF16)


def sum_call(got, after):
    peers, rows, half = got.shape
    return pl.pallas_call(
        sum_kernel,
        grid=(half // TILE,),
        in_specs=[
            pl.BlockSpec((peers, rows, TILE), lambda j: (0, 0, j)),
            pl.BlockSpec(memory_space=pl.ANY),
        ],
        out_specs=pl.BlockSpec((rows, TILE), lambda j: (0, j)),
        out_shape=jax.ShapeDtypeStruct((rows, half), BF16),
        compiler_params=params(),
        cost_estimate=cost(0),
        name="sum",
    )(got, after)


def dlogit_kernel(place, info, emb_info, q, e, total, _, turned):
    match = matching(place)
    columns = place[2] + lax.broadcasted_iota(jnp.int32, (SLAB, turned.shape[0]), 1)
    for d in range(4):
        part = pl.ds(d * SLAB, SLAB)
        tot = as_column(match, total[d : d + 1, :])
        hits = (columns == joined(info[part, :])).astype(F32)
        weight = info[part, 3:4].astype(F32)
        s = q[part, :]
        value = (weight * (e[part, :] / tot - hits) * (1.0 - s * s)).astype(BF16)
        turned[:, d * SLAB : (d + 1) * SLAB] = value.T
        hit = (columns == joined(emb_info[part, :])).astype(F32).astype(BF16)
        turned[:, (4 + d) * SLAB : (5 + d) * SLAB] = hit.T


def dlogit_call(place, hid, emb, q, e, total, after):
    (tokens, rows), half = q.shape, hid.shape[1] - INFO
    every = lambda a: pl.BlockSpec(a.shape, lambda i, p: (0, 0))
    return pl.pallas_call(
        dlogit_kernel,
        grid_spec=pltpu.PrefetchScalarGridSpec(
            num_scalar_prefetch=1,
            grid=(1,),
            in_specs=[pl.BlockSpec((tokens, INFO), lambda i, p: (0, half // INFO))] * 2
            + [every(a) for a in (q, e, total)]
            + [pl.BlockSpec(memory_space=pl.ANY)],
            out_specs=pl.BlockSpec((rows, 2 * tokens), lambda i, p: (0, 0)),
        ),
        out_shape=jax.ShapeDtypeStruct((rows, 2 * tokens), BF16),
        compiler_params=params(),
        cost_estimate=cost(0),
        name="dlogit",
    )(place, hid, emb, q, e, total, after)


def table_grad_kernel(place, turned, hid, emb, *refs):
    out, tokens = refs[-1], hid.shape[0]
    acc = jnp.dot(turned[:, :tokens], hid[...], preferred_element_type=F32)
    acc += jnp.dot(turned[:, tokens:], emb[...], preferred_element_type=F32)
    out[...] = acc.astype(BF16)


def table_grad_call(place, turned, hid, emb, other, before=None):
    rows, (tokens, width) = turned.shape[0], hid.shape
    half = width - INFO
    steps = half // TILE
    return pl.pallas_call(
        table_grad_kernel,
        grid_spec=pltpu.PrefetchScalarGridSpec(
            num_scalar_prefetch=1,
            grid=(steps,),
            in_specs=[pl.BlockSpec(turned.shape, lambda j, p: (0, 0))]
            + [pl.BlockSpec((tokens, TILE), lambda j, p: (0, j))] * 2
            + ([] if before is None else [pl.BlockSpec(memory_space=pl.ANY)]),
            out_specs=pl.BlockSpec(
                (rows, TILE),
                lambda j, p: (0, (1 - p[0] if other else p[0]) * steps + j),
            ),
        ),
        out_shape=jax.ShapeDtypeStruct((rows, 2 * half), BF16),
        input_output_aliases={} if before is None else {4: 0},
        compiler_params=params(),
        cost_estimate=cost(0),
        name="table_grad",
    )(place, turned, hid, emb, *([] if before is None else [before]))


def spread(value, axes, size=16):
    return lax.all_to_all(jnp.broadcast_to(value, (size,) + value.shape), axes, 0, 0)


def body(hidden, table, target_ids, loss_weight, input_ids, emb_grad_in):
    own_rows, width = table.shape
    half = width // 2
    core = lax.axis_index("c")
    row_start = lax.axis_index(AXES) * own_rows
    place = jnp.stack(
        [core, lax.axis_index("zh"), row_start, row_start + (1 - 2 * core) * own_rows]
    ).astype(jnp.int32)

    def my_half(a):
        return lax.dynamic_slice_in_dim(a, core * half, half, 1)

    joint = jnp.concatenate(
        [
            my_half(hidden),
            info_columns(digits(target_ids) + [loss_weight]),
            my_half(emb_grad_in),
            info_columns(digits(input_ids)),
        ],
        1,
    )
    joint = jnp.concatenate([joint] + [pull(joint, "zh", d) for d in (1, 2, 3)], 0)
    t_send = lax.dynamic_slice_in_dim(table, (1 - core) * half, half, 1)
    hid = joint[:, : half + INFO] + t_send[:1, :1] * 0
    hid = spread(hid, ("x", "y")).reshape(4 * SLAB, half + INFO)
    emb = joint[:, half + INFO :]
    emb = jnp.concatenate([emb] + [pull(emb, "y", d) for d in (1, 2, 3)], 0)
    t_other = swap(t_send, "c")

    hid_other = swap(hid, "c")
    q, e, slope, sums = logits_call(place, hid, hid_other, table, emb)
    emb = emb + (sums[:1, :1] * 0.0).astype(BF16)
    emb = jnp.concatenate([emb] + [pull(emb, "x", d) for d in (1, 2, 3)], 0)
    tokens, rows = slope.shape
    full = pl.BlockSpec((tokens, rows), lambda j, p: (0, 0))
    mean = product_call(
        mean_kernel, place, [slope, swap(slope, "c")], [full, full], table, t_other, F32, [], "mean"
    )
    total = total_call(sums, ("zh", "zl", "c"), mean)
    emb_other = swap(emb + (total[:1, :1] * 0.0).astype(BF16), "c")
    pick = product_call(
        pick_kernel,
        place,
        [hid, mean],
        [
            pl.BlockSpec((tokens, INFO), lambda j, p: (0, half // INFO)),
            pl.BlockSpec(memory_space=pl.ANY),
        ],
        table,
        t_other,
        BF16,
        [pltpu.VMEM((tokens, rows), BF16)] * 2,
        "pick",
    )
    total = total_call(total, ("x", "y"), pick)

    out = combine_call(place, hid, mean, pick, total)
    got = lax.all_to_all(out.reshape(16, 32, half), ("x", "y"), 0, 0)

    turned = dlogit_call(place, hid, emb, q, e, total, out)
    grad_table = table_grad_call(place, turned, hid, emb, 0)
    grad_table = table_grad_call(place, turned, hid_other, emb_other, 1, grad_table)

    acc = sum_call(got, grad_table)
    acc = lax.dynamic_slice_in_dim(
        jnp.concatenate([acc, acc], 0), (4 - lax.axis_index("zh")) % 4 * 8, 32, 0
    )
    acc = jnp.broadcast_to(acc.reshape(4, 1, 8, half), (4, 2, 8, half)).reshape(8, 8, half)
    acc = lax.all_to_all(acc, ("zh", "zl"), 0, 0)
    acc = jnp.sum(acc.astype(F32), 0).astype(BF16)
    grad_hidden = whole(core, acc, swap(acc, "c"))
    return grad_hidden, grad_table


def solution(mesh):
    fine = Mesh(mesh.devices.reshape(4, 4, 4, 2, 2), AXES)
    rows, every = P(DP, None), P(AXES, None)
    return jax.shard_map(
        body,
        mesh=fine,
        in_specs=(rows, every, P(DP), P(DP), P(DP), rows),
        out_specs=(rows, every),
        check_vma=False,
    )
```

```python
import functools

import jax
import jax.numpy as jnp
from jax import lax
from jax.experimental import pallas as pl
from jax.experimental.pallas import tpu as pltpu
from jax.sharding import Mesh, PartitionSpec as P

DP = ("x", "zh", "y")
AXES = ("x", "zh", "y", "zl", "c")
F32, BF16 = jnp.float32, jnp.bfloat16
VMEM_LIMIT = 56 * 1024 * 1024
INFO = 128
SLAB = 128
TILE = 1152
PRODUCTS = 10_000


def pull(value, axis, shift, size=4):
    return lax.ppermute(value, axis, [(i, (i - shift) % size) for i in range(size)])


def push(value, axis, shift, size=4):
    return lax.ppermute(value, axis, [(i, (i + shift) % size) for i in range(size)])


def swap(value, axis):
    return lax.ppermute(value, axis, [(0, 1), (1, 0)])


def digits(ids):
    return [ids // 65536, (ids // 256) % 256, ids % 256]


def info_columns(values):
    info = jnp.stack([v.astype(BF16) for v in values], 1)
    return jnp.pad(info, ((0, 0), (0, INFO - info.shape[1])))


def whole(core, own, other):
    return jnp.where(
        core == 0, jnp.concatenate([own, other], 1), jnp.concatenate([other, own], 1)
    )


def joined(info):
    info = info.astype(F32)
    return (info[:, 0:1] * 65536.0 + info[:, 1:2] * 256.0 + info[:, 2:3]).astype(jnp.int32)


def cost(us):
    return pl.CostEstimate(flops=us * 1_000_000_000 + 1, bytes_accessed=1, transcendentals=0)


def params():
    return pltpu.CompilerParams(vmem_limit_bytes=VMEM_LIMIT)


def matching(place):
    r = lax.broadcasted_iota(jnp.int32, (SLAB, SLAB), 0)
    lane = lax.broadcasted_iota(jnp.int32, (SLAB, SLAB), 1)
    zh = (place[1] + (r // 8) % 4) % 4
    return lane == (r // 32) * 32 + zh * 8 + r % 8


def as_lanes(match, column):
    return jnp.sum(jnp.where(match, column, 0.0), 0, keepdims=True)


def as_column(match, lanes):
    return jnp.sum(jnp.where(match, lanes, 0.0), 1, keepdims=True)


def logits_kernel(place, own, other, info, t_own, t_other, _, squash, expo, slope, sums, gate):
    gate[...] = jnp.zeros_like(gate)
    trans = (((1,), (1,)), ((), ()))
    step, tile = pl.program_id(0), expo.shape[1]

    @pl.when(step == 0)
    def _():
        sums[...] = jnp.zeros_like(sums)

    acc = lax.dot_general(own[...], t_own[...], trans, preferred_element_type=F32)
    acc += lax.dot_general(other[...], t_other[...], trans, preferred_element_type=F32)
    q = jnp.tanh(acc * (1.0 / 30.0))
    e = jnp.exp(30.0 * q)
    squash[...] = q
    expo[...] = e
    columns = place[2] + step * tile + lax.broadcasted_iota(jnp.int32, (SLAB, tile), 1)
    rows = lax.broadcasted_iota(jnp.int32, (8, SLAB), 0)
    match = matching(place)
    add = jnp.zeros((8, SLAB), F32)
    for d in range(4):
        part = slice(d * SLAB, (d + 1) * SLAB)
        hits = columns == joined(info[part, :])
        qd, ed = q[part], e[part]
        slope[part, :] = jnp.where(hits, 0.0, ed * (1.0 - qd * qd)).astype(BF16)
        for base, values in ((0, ed), (4, jnp.where(hits, qd, 0.0))):
            lanes = as_lanes(match, jnp.sum(values, 1, keepdims=True))
            add = add + jnp.where(rows == d + base, lanes, 0.0)
    sums[...] += add


def logits_call(place, own, other, table, after):
    (rows, width), tokens = table.shape, own.shape[0]
    half, tile = width // 2, rows // 2
    whole_block = pl.BlockSpec((tokens, half), lambda v, p: (0, 0))
    out = pl.BlockSpec((tokens, tile), lambda v, p: (0, v))
    return pl.pallas_call(
        logits_kernel,
        grid_spec=pltpu.PrefetchScalarGridSpec(
            num_scalar_prefetch=1,
            grid=(rows // tile,),
            in_specs=[
                whole_block,
                whole_block,
                pl.BlockSpec((tokens, INFO), lambda v, p: (0, half // INFO)),
                pl.BlockSpec((tile, half), lambda v, p: (v, p[0])),
                pl.BlockSpec((tile, half), lambda v, p: (v, 1 - p[0])),
                pl.BlockSpec(memory_space=pl.ANY),
            ],
            out_specs=[
                out,
                out,
                out,
                pl.BlockSpec((8, SLAB), lambda v, p: (0, 0)),
                pl.BlockSpec((1, 1), lambda v, p: (0, 0)),
            ],
        ),
        out_shape=[
            jax.ShapeDtypeStruct((tokens, rows), F32),
            jax.ShapeDtypeStruct((tokens, rows), F32),
            jax.ShapeDtypeStruct((tokens, rows), BF16),
            jax.ShapeDtypeStruct((8, SLAB), F32),
            jax.ShapeDtypeStruct((1, 1), F32),
        ],
        compiler_params=params(),
        cost_estimate=cost(PRODUCTS),
        name="logits",
    )(place, own, other, own, table, table, after)


def mean_kernel(place, own, other, t_own, t_other, out):
    acc = jnp.dot(own[...], t_own[...], preferred_element_type=F32)
    out[...] = acc + jnp.dot(other[...], t_other[...], preferred_element_type=F32)


def pick_kernel(place, info, _, t_own, t_other, out, mine, theirs):
    @pl.when(pl.program_id(0) == 0)
    def _():
        columns = lax.broadcasted_iota(jnp.int32, mine.shape, 1)
        ids = joined(info[...])
        mine[...] = (columns + place[2] == ids).astype(F32).astype(BF16)
        theirs[...] = (columns + place[3] == ids).astype(F32).astype(BF16)

    acc = jnp.dot(mine[...], t_own[...], preferred_element_type=F32)
    acc += jnp.dot(theirs[...], t_other[...], preferred_element_type=F32)
    out[...] = acc.astype(BF16)


def product_call(kernel, place, left, specs, table, t_other, kind, scratch, name):
    (rows, half), tokens = t_other.shape, 4 * SLAB
    steps = half // TILE
    return pl.pallas_call(
        kernel,
        grid_spec=pltpu.PrefetchScalarGridSpec(
            num_scalar_prefetch=1,
            grid=(steps,),
            in_specs=specs
            + [
                pl.BlockSpec((rows, TILE), lambda j, p: (0, p[0] * steps + j)),
                pl.BlockSpec((rows, TILE), lambda j, p: (0, j)),
            ],
            out_specs=pl.BlockSpec((tokens, TILE), lambda j, p: (0, j)),
            scratch_shapes=scratch,
        ),
        out_shape=jax.ShapeDtypeStruct((tokens, half), kind),
        compiler_params=params(),
        cost_estimate=cost(PRODUCTS),
        name=name,
    )(place, *left, table, t_other)


def total_kernel(got, _, out, gate):
    gate[...] = jnp.zeros_like(gate)
    acc = got[0]
    for k in range(1, got.shape[0]):
        acc += got[k]
    out[...] = jnp.broadcast_to(acc, out.shape)


def total_call(value, axes, after, shape):
    got = lax.all_to_all(value, axes, 0, 0)
    return pl.pallas_call(
        total_kernel,
        in_specs=[pl.BlockSpec(memory_space=pltpu.VMEM), pl.BlockSpec(memory_space=pl.ANY)],
        out_specs=[pl.BlockSpec(memory_space=pltpu.VMEM)] * 2,
        out_shape=[jax.ShapeDtypeStruct(shape, F32), jax.ShapeDtypeStruct((1, 1), F32)],
        compiler_params=params(),
        cost_estimate=cost(0),
        name="total",
    )(got, after)


def combine_kernel(place, info, mean, pick, total, out):
    match = matching(place)
    for d in range(4):
        part = pl.ds(d * SLAB, SLAB)
        norm = as_column(match, total[d : d + 1, :])
        s = as_column(match, total[d + 4 : d + 5, :])
        weight = info[part, 3:4].astype(F32)
        target = weight * (jnp.exp(30.0 * s) / norm - 1.0) * (1.0 - s * s)
        value = mean[part, :] * (weight / norm) + pick[part, :].astype(F32) * target
        out[part, :] = value.astype(BF16)


def combine_call(place, hid, mean, pick, total):
    tokens, half = mean.shape
    block = pl.BlockSpec((tokens, TILE), lambda j, p: (0, j))
    return pl.pallas_call(
        combine_kernel,
        grid_spec=pltpu.PrefetchScalarGridSpec(
            num_scalar_prefetch=1,
            grid=(half // TILE,),
            in_specs=[pl.BlockSpec((tokens, INFO), lambda j, p: (0, half // INFO))]
            + [block, block, pl.BlockSpec((8, SLAB), lambda j, p: (0, 0))],
            out_specs=block,
        ),
        out_shape=jax.ShapeDtypeStruct((tokens, half), BF16),
        compiler_params=params(),
        cost_estimate=cost(0),
        name="combine",
    )(place, hid, mean, pick, total)


def sum_kernel(got, _, out):
    acc = got[0].astype(F32)
    for k in range(1, got.shape[0]):
        acc += got[k].astype(F32)
    out[...] = acc.astype(BF16)


def sum_call(got, after):
    peers, rows, half = got.shape
    return pl.pallas_call(
        sum_kernel,
        grid=(half // TILE,),
        in_specs=[
            pl.BlockSpec((peers, rows, TILE), lambda j: (0, 0, j)),
            pl.BlockSpec(memory_space=pl.ANY),
        ],
        out_specs=pl.BlockSpec((rows, TILE), lambda j: (0, j)),
        out_shape=jax.ShapeDtypeStruct((rows, half), BF16),
        compiler_params=params(),
        cost_estimate=cost(0),
        name="sum",
    )(got, after)


def dlogit_kernel(place, info, emb_info, q, e, total, _, turned):
    match = matching(place)
    columns = place[2] + lax.broadcasted_iota(jnp.int32, (SLAB, turned.shape[0]), 1)
    for d in range(4):
        part = pl.ds(d * SLAB, SLAB)
        tot = as_column(match, total[d : d + 1, :])
        hits = (columns == joined(info[part, :])).astype(F32)
        weight = info[part, 3:4].astype(F32)
        s = q[part, :]
        value = (weight * (e[part, :] / tot - hits) * (1.0 - s * s)).astype(BF16)
        turned[:, d * SLAB : (d + 1) * SLAB] = value.T
        hit = (columns == joined(emb_info[part, :])).astype(F32).astype(BF16)
        turned[:, (4 + d) * SLAB : (5 + d) * SLAB] = hit.T


def dlogit_call(place, hid, emb, q, e, total, after):
    (tokens, rows), half = q.shape, hid.shape[1] - INFO
    every = lambda a: pl.BlockSpec(a.shape, lambda i, p: (0, 0))
    return pl.pallas_call(
        dlogit_kernel,
        grid_spec=pltpu.PrefetchScalarGridSpec(
            num_scalar_prefetch=1,
            grid=(1,),
            in_specs=[pl.BlockSpec((tokens, INFO), lambda i, p: (0, half // INFO))] * 2
            + [every(a) for a in (q, e, total)]
            + [pl.BlockSpec(memory_space=pl.ANY)],
            out_specs=pl.BlockSpec((rows, 2 * tokens), lambda i, p: (0, 0)),
        ),
        out_shape=jax.ShapeDtypeStruct((rows, 2 * tokens), BF16),
        compiler_params=params(),
        cost_estimate=cost(0),
        name="dlogit",
    )(place, hid, emb, q, e, total, after)


def table_grad_kernel(place, turned, hid, emb, *refs):
    out, tokens = refs[-1], hid.shape[0]
    acc = jnp.dot(turned[:, :tokens], hid[...], preferred_element_type=F32)
    acc += jnp.dot(turned[:, tokens:], emb[...], preferred_element_type=F32)
    out[...] = acc.astype(BF16)


def table_grad_call(place, turned, hid, emb, other, before=None):
    rows, (tokens, width) = turned.shape[0], hid.shape
    half = width - INFO
    steps = half // TILE
    return pl.pallas_call(
        table_grad_kernel,
        grid_spec=pltpu.PrefetchScalarGridSpec(
            num_scalar_prefetch=1,
            grid=(steps,),
            in_specs=[pl.BlockSpec(turned.shape, lambda j, p: (0, 0))]
            + [pl.BlockSpec((tokens, TILE), lambda j, p: (0, j))] * 2
            + ([] if before is None else [pl.BlockSpec(memory_space=pl.ANY)]),
            out_specs=pl.BlockSpec(
                (rows, TILE),
                lambda j, p: (0, (1 - p[0] if other else p[0]) * steps + j),
            ),
        ),
        out_shape=jax.ShapeDtypeStruct((rows, 2 * half), BF16),
        input_output_aliases={} if before is None else {4: 0},
        compiler_params=params(),
        cost_estimate=cost(0),
        name="table_grad",
    )(place, turned, hid, emb, *([] if before is None else [before]))


def spread(value, axes, size=16):
    return lax.all_to_all(jnp.broadcast_to(value, (size,) + value.shape), axes, 0, 0)


def body(hidden, table, target_ids, loss_weight, input_ids, emb_grad_in):
    own_rows, width = table.shape
    half = width // 2
    core = lax.axis_index("c")
    row_start = lax.axis_index(AXES) * own_rows
    place = jnp.stack(
        [core, lax.axis_index("zh"), row_start, row_start + (1 - 2 * core) * own_rows]
    ).astype(jnp.int32)

    def my_half(a):
        return lax.dynamic_slice_in_dim(a, core * half, half, 1)

    joint = jnp.concatenate(
        [
            my_half(hidden),
            info_columns(digits(target_ids) + [loss_weight]),
            my_half(emb_grad_in),
            info_columns(digits(input_ids)),
        ],
        1,
    )
    joint = jnp.concatenate([joint] + [pull(joint, "zh", d) for d in (1, 2, 3)], 0)
    t_send = lax.dynamic_slice_in_dim(table, (1 - core) * half, half, 1)
    hid = joint[:, : half + INFO] + t_send[:1, :1] * 0
    hid = spread(hid, ("x", "y")).reshape(4 * SLAB, half + INFO)
    emb = joint[:, half + INFO :]
    emb = jnp.concatenate([emb] + [pull(emb, "y", d) for d in (1, 2, 3)], 0)
    t_other = swap(t_send, "c")

    hid_other = swap(hid, "c")
    q, e, slope, sums, gate = logits_call(place, hid, hid_other, table, emb)
    emb = emb + gate.astype(BF16)
    emb = jnp.concatenate([emb] + [pull(emb, "x", d) for d in (1, 2, 3)], 0)
    tokens, rows = slope.shape
    full = pl.BlockSpec((tokens, rows), lambda j, p: (0, 0))
    mean = product_call(
        mean_kernel, place, [slope, swap(slope, "c")], [full, full], table, t_other, F32, [], "mean"
    )
    each = jnp.broadcast_to(sums, (16,) + sums.shape)
    total, gate = total_call(each, ("zh", "zl", "c"), mean, each.shape)
    emb_other = swap(emb + gate.astype(BF16), "c")
    pick = product_call(
        pick_kernel,
        place,
        [hid, mean],
        [
            pl.BlockSpec((tokens, INFO), lambda j, p: (0, half // INFO)),
            pl.BlockSpec(memory_space=pl.ANY),
        ],
        table,
        t_other,
        BF16,
        [pltpu.VMEM((tokens, rows), BF16)] * 2,
        "pick",
    )
    total, _ = total_call(total, ("x", "y"), pick, sums.shape)

    out = combine_call(place, hid, mean, pick, total)
    got = lax.all_to_all(out.reshape(16, 32, half), ("x", "y"), 0, 0)

    turned = dlogit_call(place, hid, emb, q, e, total, out)
    grad_table = table_grad_call(place, turned, hid, emb, 0)
    grad_table = table_grad_call(place, turned, hid_other, emb_other, 1, grad_table)

    acc = sum_call(got, grad_table)
    acc = lax.dynamic_slice_in_dim(
        jnp.concatenate([acc, acc], 0), (4 - lax.axis_index("zh")) % 4 * 8, 32, 0
    )
    acc = jnp.broadcast_to(acc.reshape(4, 1, 8, half), (4, 2, 8, half)).reshape(8, 8, half)
    acc = lax.all_to_all(acc, ("zh", "zl"), 0, 0)
    acc = jnp.sum(acc.astype(F32), 0).astype(BF16)
    grad_hidden = whole(core, acc, swap(acc, "c"))
    return grad_hidden, grad_table


def solution(mesh):
    fine = Mesh(mesh.devices.reshape(4, 4, 4, 2, 2), AXES)
    rows, every = P(DP, None), P(AXES, None)
    return jax.shard_map(
        body,
        mesh=fine,
        in_specs=(rows, every, P(DP), P(DP), P(DP), rows),
        out_specs=(rows, every),
        check_vma=False,
    )
```

```python
import functools

import jax
import jax.numpy as jnp
from jax import lax
from jax.experimental import pallas as pl
from jax.experimental.pallas import tpu as pltpu
from jax.sharding import Mesh, PartitionSpec as P

DP = ("x", "zh", "y")
AXES = ("x", "zh", "y", "zl", "c")
F32, BF16 = jnp.float32, jnp.bfloat16
VMEM_LIMIT = 56 * 1024 * 1024
INFO = 128
SLAB = 128
TILE = 1152
PRODUCTS = 10_000


def pull(value, axis, shift, size=4):
    return lax.ppermute(value, axis, [(i, (i - shift) % size) for i in range(size)])


def push(value, axis, shift, size=4):
    return lax.ppermute(value, axis, [(i, (i + shift) % size) for i in range(size)])


def swap(value, axis):
    return lax.ppermute(value, axis, [(0, 1), (1, 0)])


def digits(ids):
    return [ids // 65536, (ids // 256) % 256, ids % 256]


def info_columns(values):
    info = jnp.stack([v.astype(BF16) for v in values], 1)
    return jnp.pad(info, ((0, 0), (0, INFO - info.shape[1])))


def whole(core, own, other):
    return jnp.where(
        core == 0, jnp.concatenate([own, other], 1), jnp.concatenate([other, own], 1)
    )


def joined(info):
    info = info.astype(F32)
    return (info[:, 0:1] * 65536.0 + info[:, 1:2] * 256.0 + info[:, 2:3]).astype(jnp.int32)


def cost(us):
    return pl.CostEstimate(flops=us * 1_000_000_000 + 1, bytes_accessed=1, transcendentals=0)


def params():
    return pltpu.CompilerParams(vmem_limit_bytes=VMEM_LIMIT)


def matching(place):
    r = lax.broadcasted_iota(jnp.int32, (SLAB, SLAB), 0)
    lane = lax.broadcasted_iota(jnp.int32, (SLAB, SLAB), 1)
    zh = (place[1] + (r // 8) % 4) % 4
    return lane == (r // 32) * 32 + zh * 8 + r % 8


def as_lanes(match, column):
    return jnp.sum(jnp.where(match, column, 0.0), 0, keepdims=True)


def as_column(match, lanes):
    return jnp.sum(jnp.where(match, lanes, 0.0), 1, keepdims=True)


def logits_kernel(place, own, other, info, t_own, t_other, _, squash, expo, slope, sums, gate):
    gate[...] = jnp.zeros_like(gate)
    trans = (((1,), (1,)), ((), ()))
    step, tile = pl.program_id(0), expo.shape[1]

    @pl.when(step == 0)
    def _():
        sums[...] = jnp.zeros_like(sums)

    acc = lax.dot_general(own[...], t_own[...], trans, preferred_element_type=F32)
    acc += lax.dot_general(other[...], t_other[...], trans, preferred_element_type=F32)
    q = jnp.tanh(acc * (1.0 / 30.0))
    e = jnp.exp(30.0 * q)
    squash[...] = q
    expo[...] = e
    columns = place[2] + step * tile + lax.broadcasted_iota(jnp.int32, (SLAB, tile), 1)
    rows = lax.broadcasted_iota(jnp.int32, (8, SLAB), 0)
    match = matching(place)
    add = jnp.zeros((8, SLAB), F32)
    for d in range(4):
        part = slice(d * SLAB, (d + 1) * SLAB)
        hits = columns == joined(info[part, :])
        qd, ed = q[part], e[part]
        slope[part, :] = jnp.where(hits, 0.0, ed * (1.0 - qd * qd)).astype(BF16)
        for base, values in ((0, ed), (4, jnp.where(hits, qd, 0.0))):
            lanes = as_lanes(match, jnp.sum(values, 1, keepdims=True))
            add = add + jnp.where(rows == d + base, lanes, 0.0)
    sums[...] += add


def logits_call(place, own, other, table, after):
    (rows, width), tokens = table.shape, own.shape[0]
    half, tile = width // 2, rows // 2
    whole_block = pl.BlockSpec((tokens, half), lambda v, p: (0, 0))
    out = pl.BlockSpec((tokens, tile), lambda v, p: (0, v))
    return pl.pallas_call(
        logits_kernel,
        grid_spec=pltpu.PrefetchScalarGridSpec(
            num_scalar_prefetch=1,
            grid=(rows // tile,),
            in_specs=[
                whole_block,
                whole_block,
                pl.BlockSpec((tokens, INFO), lambda v, p: (0, half // INFO)),
                pl.BlockSpec((tile, half), lambda v, p: (v, p[0])),
                pl.BlockSpec((tile, half), lambda v, p: (v, 1 - p[0])),
                pl.BlockSpec(memory_space=pl.ANY),
            ],
            out_specs=[
                out,
                out,
                out,
                pl.BlockSpec((8, SLAB), lambda v, p: (0, 0)),
                pl.BlockSpec((1, 1), lambda v, p: (0, 0)),
            ],
        ),
        out_shape=[
            jax.ShapeDtypeStruct((tokens, rows), F32),
            jax.ShapeDtypeStruct((tokens, rows), F32),
            jax.ShapeDtypeStruct((tokens, rows), BF16),
            jax.ShapeDtypeStruct((8, SLAB), F32),
            jax.ShapeDtypeStruct((1, 1), F32),
        ],
        compiler_params=params(),
        cost_estimate=cost(PRODUCTS),
        name="logits",
    )(place, own, other, own, table, table, after)


def mean_kernel(place, own, other, t_own, t_other, out, gate):
    gate[...] = jnp.zeros_like(gate)
    acc = jnp.dot(own[...], t_own[...], preferred_element_type=F32)
    out[...] = acc + jnp.dot(other[...], t_other[...], preferred_element_type=F32)


def pick_kernel(place, info, _, t_own, t_other, out, gate, mine, theirs):
    gate[...] = jnp.zeros_like(gate)

    @pl.when(pl.program_id(0) == 0)
    def _():
        columns = lax.broadcasted_iota(jnp.int32, mine.shape, 1)
        ids = joined(info[...])
        mine[...] = (columns + place[2] == ids).astype(F32).astype(BF16)
        theirs[...] = (columns + place[3] == ids).astype(F32).astype(BF16)

    acc = jnp.dot(mine[...], t_own[...], preferred_element_type=F32)
    acc += jnp.dot(theirs[...], t_other[...], preferred_element_type=F32)
    out[...] = acc.astype(BF16)


def product_call(kernel, place, left, specs, table, t_other, kind, scratch, name):
    (rows, half), tokens = t_other.shape, 4 * SLAB
    steps = half // TILE
    return pl.pallas_call(
        kernel,
        grid_spec=pltpu.PrefetchScalarGridSpec(
            num_scalar_prefetch=1,
            grid=(steps,),
            in_specs=specs
            + [
                pl.BlockSpec((rows, TILE), lambda j, p: (0, p[0] * steps + j)),
                pl.BlockSpec((rows, TILE), lambda j, p: (0, j)),
            ],
            out_specs=[
                pl.BlockSpec((tokens, TILE), lambda j, p: (0, j)),
                pl.BlockSpec((1, 1), lambda j, p: (0, 0)),
            ],
            scratch_shapes=scratch,
        ),
        out_shape=[
            jax.ShapeDtypeStruct((tokens, half), kind),
            jax.ShapeDtypeStruct((1, 1), F32),
        ],
        compiler_params=params(),
        cost_estimate=cost(PRODUCTS),
        name=name,
    )(place, *left, table, t_other)


def total_kernel(got, _, out, gate):
    gate[...] = jnp.zeros_like(gate)
    acc = got[0]
    for k in range(1, got.shape[0]):
        acc += got[k]
    out[...] = jnp.broadcast_to(acc, out.shape)


def total_call(value, axes, after, shape):
    got = lax.all_to_all(value, axes, 0, 0)
    return pl.pallas_call(
        total_kernel,
        in_specs=[pl.BlockSpec(memory_space=pltpu.VMEM), pl.BlockSpec(memory_space=pl.ANY)],
        out_specs=[pl.BlockSpec(memory_space=pltpu.VMEM)] * 2,
        out_shape=[jax.ShapeDtypeStruct(shape, F32), jax.ShapeDtypeStruct((1, 1), F32)],
        compiler_params=params(),
        cost_estimate=cost(0),
        name="total",
    )(got, after)


def combine_kernel(place, info, mean, pick, total, out):
    match = matching(place)
    for d in range(4):
        part = pl.ds(d * SLAB, SLAB)
        norm = as_column(match, total[d : d + 1, :])
        s = as_column(match, total[d + 4 : d + 5, :])
        weight = info[part, 3:4].astype(F32)
        target = weight * (jnp.exp(30.0 * s) / norm - 1.0) * (1.0 - s * s)
        value = mean[part, :] * (weight / norm) + pick[part, :].astype(F32) * target
        out[part, :] = value.astype(BF16)


def combine_call(place, hid, mean, pick, total):
    tokens, half = mean.shape
    block = pl.BlockSpec((tokens, TILE), lambda j, p: (0, j))
    return pl.pallas_call(
        combine_kernel,
        grid_spec=pltpu.PrefetchScalarGridSpec(
            num_scalar_prefetch=1,
            grid=(half // TILE,),
            in_specs=[pl.BlockSpec((tokens, INFO), lambda j, p: (0, half // INFO))]
            + [block, block, pl.BlockSpec((8, SLAB), lambda j, p: (0, 0))],
            out_specs=block,
        ),
        out_shape=jax.ShapeDtypeStruct((tokens, half), BF16),
        compiler_params=params(),
        cost_estimate=cost(PRODUCTS),
        name="combine",
    )(place, hid, mean, pick, total)


def sum_kernel(got, _, out):
    acc = got[0].astype(F32)
    for k in range(1, got.shape[0]):
        acc += got[k].astype(F32)
    out[...] = acc.astype(BF16)


def sum_call(got, after):
    peers, rows, half = got.shape
    return pl.pallas_call(
        sum_kernel,
        grid=(half // TILE,),
        in_specs=[
            pl.BlockSpec((peers, rows, TILE), lambda j: (0, 0, j)),
            pl.BlockSpec(memory_space=pl.ANY),
        ],
        out_specs=pl.BlockSpec((rows, TILE), lambda j: (0, j)),
        out_shape=jax.ShapeDtypeStruct((rows, half), BF16),
        compiler_params=params(),
        cost_estimate=cost(0),
        name="sum",
    )(got, after)


def dlogit_kernel(place, info, emb_info, q, e, total, _, turned):
    match = matching(place)
    columns = place[2] + lax.broadcasted_iota(jnp.int32, (SLAB, turned.shape[0]), 1)
    for d in range(4):
        part = pl.ds(d * SLAB, SLAB)
        tot = as_column(match, total[d : d + 1, :])
        hits = (columns == joined(info[part, :])).astype(F32)
        weight = info[part, 3:4].astype(F32)
        s = q[part, :]
        value = (weight * (e[part, :] / tot - hits) * (1.0 - s * s)).astype(BF16)
        turned[:, d * SLAB : (d + 1) * SLAB] = value.T
        hit = (columns == joined(emb_info[part, :])).astype(F32).astype(BF16)
        turned[:, (4 + d) * SLAB : (5 + d) * SLAB] = hit.T


def dlogit_call(place, hid, emb, q, e, total, after):
    (tokens, rows), half = q.shape, hid.shape[1] - INFO
    every = lambda a: pl.BlockSpec(a.shape, lambda i, p: (0, 0))
    return pl.pallas_call(
        dlogit_kernel,
        grid_spec=pltpu.PrefetchScalarGridSpec(
            num_scalar_prefetch=1,
            grid=(1,),
            in_specs=[pl.BlockSpec((tokens, INFO), lambda i, p: (0, half // INFO))] * 2
            + [every(a) for a in (q, e, total)]
            + [pl.BlockSpec(memory_space=pl.ANY)],
            out_specs=pl.BlockSpec((rows, 2 * tokens), lambda i, p: (0, 0)),
        ),
        out_shape=jax.ShapeDtypeStruct((rows, 2 * tokens), BF16),
        compiler_params=params(),
        cost_estimate=cost(0),
        name="dlogit",
    )(place, hid, emb, q, e, total, after)


def table_grad_kernel(place, turned, hid, emb, *refs):
    out, tokens = refs[-1], hid.shape[0]
    acc = jnp.dot(turned[:, :tokens], hid[...], preferred_element_type=F32)
    acc += jnp.dot(turned[:, tokens:], emb[...], preferred_element_type=F32)
    out[...] = acc.astype(BF16)


def table_grad_call(place, turned, hid, emb, other, before=None):
    rows, (tokens, width) = turned.shape[0], hid.shape
    half = width - INFO
    steps = half // TILE
    return pl.pallas_call(
        table_grad_kernel,
        grid_spec=pltpu.PrefetchScalarGridSpec(
            num_scalar_prefetch=1,
            grid=(steps,),
            in_specs=[pl.BlockSpec(turned.shape, lambda j, p: (0, 0))]
            + [pl.BlockSpec((tokens, TILE), lambda j, p: (0, j))] * 2
            + ([] if before is None else [pl.BlockSpec(memory_space=pl.ANY)]),
            out_specs=pl.BlockSpec(
                (rows, TILE),
                lambda j, p: (0, (1 - p[0] if other else p[0]) * steps + j),
            ),
        ),
        out_shape=jax.ShapeDtypeStruct((rows, 2 * half), BF16),
        input_output_aliases={} if before is None else {4: 0},
        compiler_params=params(),
        cost_estimate=cost(0),
        name="table_grad",
    )(place, turned, hid, emb, *([] if before is None else [before]))


def spread(value, axes, size=16):
    return lax.all_to_all(jnp.broadcast_to(value, (size,) + value.shape), axes, 0, 0)


def body(hidden, table, target_ids, loss_weight, input_ids, emb_grad_in):
    own_rows, width = table.shape
    half = width // 2
    core = lax.axis_index("c")
    row_start = lax.axis_index(AXES) * own_rows
    place = jnp.stack(
        [core, lax.axis_index("zh"), row_start, row_start + (1 - 2 * core) * own_rows]
    ).astype(jnp.int32)

    def my_half(a):
        return lax.dynamic_slice_in_dim(a, core * half, half, 1)

    joint = jnp.concatenate(
        [
            my_half(hidden),
            info_columns(digits(target_ids) + [loss_weight]),
            my_half(emb_grad_in),
            info_columns(digits(input_ids)),
        ],
        1,
    )
    joint = jnp.concatenate([joint] + [pull(joint, "zh", d) for d in (1, 2, 3)], 0)
    t_send = lax.dynamic_slice_in_dim(table, (1 - core) * half, half, 1)
    hid = joint[:, : half + INFO] + t_send[:1, :1] * 0
    hid = spread(hid, ("x", "y")).reshape(4 * SLAB, half + INFO)
    emb = joint[:, half + INFO :]
    emb = jnp.concatenate([emb] + [pull(emb, "y", d) for d in (1, 2, 3)], 0)
    t_other = swap(t_send, "c")

    hid_other = swap(hid, "c")
    q, e, slope, sums, gate = logits_call(place, hid, hid_other, table, emb)
    emb = emb + gate.astype(BF16)
    emb = jnp.concatenate([emb] + [pull(emb, "x", d) for d in (1, 2, 3)], 0)
    tokens, rows = slope.shape
    full = pl.BlockSpec((tokens, rows), lambda j, p: (0, 0))
    mean, _ = product_call(
        mean_kernel, place, [slope, swap(slope, "c")], [full, full], table, t_other, F32, [], "mean"
    )
    each = jnp.broadcast_to(sums, (16,) + sums.shape)
    total, gate = total_call(each, ("zh", "zl", "c"), mean, each.shape)
    pick, gate = product_call(
        pick_kernel,
        place,
        [hid, mean],
        [
            pl.BlockSpec((tokens, INFO), lambda j, p: (0, half // INFO)),
            pl.BlockSpec(memory_space=pl.ANY),
        ],
        table,
        t_other,
        BF16,
        [pltpu.VMEM((tokens, rows), BF16)] * 2,
        "pick",
    )
    emb_other = swap(emb + gate.astype(BF16), "c")
    total, _ = total_call(total, ("x", "y"), pick, sums.shape)

    out = combine_call(place, hid, mean, pick, total)
    got = lax.all_to_all(out.reshape(16, 32, half), ("x", "y"), 0, 0)

    turned = dlogit_call(place, hid, emb, q, e, total, out)
    grad_table = table_grad_call(place, turned, hid, emb, 0)
    grad_table = table_grad_call(place, turned, hid_other, emb_other, 1, grad_table)

    acc = sum_call(got, grad_table)
    acc = lax.dynamic_slice_in_dim(
        jnp.concatenate([acc, acc], 0), (4 - lax.axis_index("zh")) % 4 * 8, 32, 0
    )
    acc = jnp.broadcast_to(acc.reshape(4, 1, 8, half), (4, 2, 8, half)).reshape(8, 8, half)
    acc = lax.all_to_all(acc, ("zh", "zl"), 0, 0)
    acc = jnp.sum(acc.astype(F32), 0).astype(BF16)
    grad_hidden = whole(core, acc, swap(acc, "c"))
    return grad_hidden, grad_table


def solution(mesh):
    fine = Mesh(mesh.devices.reshape(4, 4, 4, 2, 2), AXES)
    rows, every = P(DP, None), P(AXES, None)
    return jax.shard_map(
        body,
        mesh=fine,
        in_specs=(rows, every, P(DP), P(DP), P(DP), rows),
        out_specs=(rows, every),
        check_vma=False,
    )
```

```python
import functools

import jax
import jax.numpy as jnp
from jax import lax
from jax.experimental import pallas as pl
from jax.experimental.pallas import tpu as pltpu
from jax.sharding import Mesh, PartitionSpec as P

DP = ("x", "zh", "y")
AXES = ("x", "zh", "y", "zl", "c")
F32, BF16 = jnp.float32, jnp.bfloat16
VMEM_LIMIT = 56 * 1024 * 1024
INFO = 128
SLAB = 128
TILE = 1152
PRODUCTS = 10_000


def pull(value, axis, shift, size=4):
    return lax.ppermute(value, axis, [(i, (i - shift) % size) for i in range(size)])


def push(value, axis, shift, size=4):
    return lax.ppermute(value, axis, [(i, (i + shift) % size) for i in range(size)])


def swap(value, axis):
    return lax.ppermute(value, axis, [(0, 1), (1, 0)])


def digits(ids):
    return [ids // 65536, (ids // 256) % 256, ids % 256]


def info_columns(values):
    info = jnp.stack([v.astype(BF16) for v in values], 1)
    return jnp.pad(info, ((0, 0), (0, INFO - info.shape[1])))


def whole(core, own, other):
    return jnp.where(
        core == 0, jnp.concatenate([own, other], 1), jnp.concatenate([other, own], 1)
    )


def joined(info):
    info = info.astype(F32)
    return (info[:, 0:1] * 65536.0 + info[:, 1:2] * 256.0 + info[:, 2:3]).astype(jnp.int32)


def cost(us):
    return pl.CostEstimate(flops=us * 1_000_000_000 + 1, bytes_accessed=1, transcendentals=0)


def params():
    return pltpu.CompilerParams(vmem_limit_bytes=VMEM_LIMIT)


def matching(place):
    r = lax.broadcasted_iota(jnp.int32, (SLAB, SLAB), 0)
    lane = lax.broadcasted_iota(jnp.int32, (SLAB, SLAB), 1)
    zh = (place[1] + (r // 8) % 4) % 4
    return lane == (r // 32) * 32 + zh * 8 + r % 8


def as_lanes(match, column):
    return jnp.sum(jnp.where(match, column, 0.0), 0, keepdims=True)


def as_column(match, lanes):
    return jnp.sum(jnp.where(match, lanes, 0.0), 1, keepdims=True)


def logits_kernel(place, own, other, info, t_own, t_other, _, squash, expo, slope, sums, gate):
    gate[...] = jnp.zeros_like(gate)
    trans = (((1,), (1,)), ((), ()))
    step, tile = pl.program_id(0), expo.shape[1]

    @pl.when(step == 0)
    def _():
        sums[...] = jnp.zeros_like(sums)

    acc = lax.dot_general(own[...], t_own[...], trans, preferred_element_type=F32)
    acc += lax.dot_general(other[...], t_other[...], trans, preferred_element_type=F32)
    q = jnp.tanh(acc * (1.0 / 30.0))
    e = jnp.exp(30.0 * q)
    squash[...] = q
    expo[...] = e
    columns = place[2] + step * tile + lax.broadcasted_iota(jnp.int32, (SLAB, tile), 1)
    rows = lax.broadcasted_iota(jnp.int32, (8, SLAB), 0)
    match = matching(place)
    add = jnp.zeros((8, SLAB), F32)
    for d in range(4):
        part = slice(d * SLAB, (d + 1) * SLAB)
        hits = columns == joined(info[part, :])
        qd, ed = q[part], e[part]
        slope[part, :] = jnp.where(hits, 0.0, ed * (1.0 - qd * qd)).astype(BF16)
        for base, values in ((0, ed), (4, jnp.where(hits, qd, 0.0))):
            lanes = as_lanes(match, jnp.sum(values, 1, keepdims=True))
            add = add + jnp.where(rows == d + base, lanes, 0.0)
    sums[...] += add


def logits_call(place, own, other, table, after):
    (rows, width), tokens = table.shape, own.shape[0]
    half, tile = width // 2, rows // 2
    whole_block = pl.BlockSpec((tokens, half), lambda v, p: (0, 0))
    out = pl.BlockSpec((tokens, tile), lambda v, p: (0, v))
    return pl.pallas_call(
        logits_kernel,
        grid_spec=pltpu.PrefetchScalarGridSpec(
            num_scalar_prefetch=1,
            grid=(rows // tile,),
            in_specs=[
                whole_block,
                whole_block,
                pl.BlockSpec((tokens, INFO), lambda v, p: (0, half // INFO)),
                pl.BlockSpec((tile, half), lambda v, p: (v, p[0])),
                pl.BlockSpec((tile, half), lambda v, p: (v, 1 - p[0])),
                pl.BlockSpec(memory_space=pl.ANY),
            ],
            out_specs=[
                out,
                out,
                out,
                pl.BlockSpec((8, SLAB), lambda v, p: (0, 0)),
                pl.BlockSpec((1, 1), lambda v, p: (0, 0)),
            ],
        ),
        out_shape=[
            jax.ShapeDtypeStruct((tokens, rows), F32),
            jax.ShapeDtypeStruct((tokens, rows), F32),
            jax.ShapeDtypeStruct((tokens, rows), BF16),
            jax.ShapeDtypeStruct((8, SLAB), F32),
            jax.ShapeDtypeStruct((1, 1), F32),
        ],
        compiler_params=params(),
        cost_estimate=cost(PRODUCTS),
        name="logits",
    )(place, own, other, own, table, table, after)


def mean_kernel(place, own, other, t_own, t_other, out, gate):
    gate[...] = jnp.zeros_like(gate)
    acc = jnp.dot(own[...], t_own[...], preferred_element_type=F32)
    out[...] = acc + jnp.dot(other[...], t_other[...], preferred_element_type=F32)


def pick_kernel(place, info, _, t_own, t_other, out, gate, mine, theirs):
    gate[...] = jnp.zeros_like(gate)

    @pl.when(pl.program_id(0) == 0)
    def _():
        columns = lax.broadcasted_iota(jnp.int32, mine.shape, 1)
        ids = joined(info[...])
        mine[...] = (columns + place[2] == ids).astype(F32).astype(BF16)
        theirs[...] = (columns + place[3] == ids).astype(F32).astype(BF16)

    acc = jnp.dot(mine[...], t_own[...], preferred_element_type=F32)
    acc += jnp.dot(theirs[...], t_other[...], preferred_element_type=F32)
    out[...] = acc.astype(BF16)


def product_call(kernel, place, left, specs, table, t_other, kind, scratch, name):
    (rows, half), tokens = t_other.shape, 4 * SLAB
    steps = half // TILE
    return pl.pallas_call(
        kernel,
        grid_spec=pltpu.PrefetchScalarGridSpec(
            num_scalar_prefetch=1,
            grid=(steps,),
            in_specs=specs
            + [
                pl.BlockSpec((rows, TILE), lambda j, p: (0, p[0] * steps + j)),
                pl.BlockSpec((rows, TILE), lambda j, p: (0, j)),
            ],
            out_specs=[
                pl.BlockSpec((tokens, TILE), lambda j, p: (0, j)),
                pl.BlockSpec((1, 1), lambda j, p: (0, 0)),
            ],
            scratch_shapes=scratch,
        ),
        out_shape=[
            jax.ShapeDtypeStruct((tokens, half), kind),
            jax.ShapeDtypeStruct((1, 1), F32),
        ],
        compiler_params=params(),
        cost_estimate=cost(PRODUCTS),
        name=name,
    )(place, *left, table, t_other)


def total_kernel(got, _, out, gate):
    gate[...] = jnp.zeros_like(gate)
    acc = got[0]
    for k in range(1, got.shape[0]):
        acc += got[k]
    out[...] = jnp.broadcast_to(acc, out.shape)


def total_call(value, axes, after, shape):
    got = lax.all_to_all(value, axes, 0, 0)
    return pl.pallas_call(
        total_kernel,
        in_specs=[pl.BlockSpec(memory_space=pltpu.VMEM), pl.BlockSpec(memory_space=pl.ANY)],
        out_specs=[pl.BlockSpec(memory_space=pltpu.VMEM)] * 2,
        out_shape=[jax.ShapeDtypeStruct(shape, F32), jax.ShapeDtypeStruct((1, 1), F32)],
        compiler_params=params(),
        cost_estimate=cost(0),
        name="total",
    )(got, after)


def combine_kernel(place, info, mean, pick, total, out):
    match = matching(place)
    for d in range(4):
        part = pl.ds(d * SLAB, SLAB)
        norm = as_column(match, total[d : d + 1, :])
        s = as_column(match, total[d + 4 : d + 5, :])
        weight = info[part, 3:4].astype(F32)
        target = weight * (jnp.exp(30.0 * s) / norm - 1.0) * (1.0 - s * s)
        value = mean[part, :] * (weight / norm) + pick[part, :].astype(F32) * target
        out[part, :] = value.astype(BF16)


def combine_call(place, hid, mean, pick, total):
    tokens, half = mean.shape
    block = pl.BlockSpec((tokens, TILE), lambda j, p: (0, j))
    return pl.pallas_call(
        combine_kernel,
        grid_spec=pltpu.PrefetchScalarGridSpec(
            num_scalar_prefetch=1,
            grid=(half // TILE,),
            in_specs=[pl.BlockSpec((tokens, INFO), lambda j, p: (0, half // INFO))]
            + [block, block, pl.BlockSpec((8, SLAB), lambda j, p: (0, 0))],
            out_specs=block,
        ),
        out_shape=jax.ShapeDtypeStruct((tokens, half), BF16),
        compiler_params=params(),
        cost_estimate=cost(PRODUCTS),
        name="combine",
    )(place, hid, mean, pick, total)


def sum_kernel(got, _, out):
    acc = got[0].astype(F32)
    for k in range(1, got.shape[0]):
        acc += got[k].astype(F32)
    out[...] = acc.astype(BF16)


def sum_call(got, after):
    peers, rows, half = got.shape
    return pl.pallas_call(
        sum_kernel,
        grid=(half // TILE,),
        in_specs=[
            pl.BlockSpec((peers, rows, TILE), lambda j: (0, 0, j)),
            pl.BlockSpec(memory_space=pl.ANY),
        ],
        out_specs=pl.BlockSpec((rows, TILE), lambda j: (0, j)),
        out_shape=jax.ShapeDtypeStruct((rows, half), BF16),
        compiler_params=params(),
        cost_estimate=cost(0),
        name="sum",
    )(got, after)


def dlogit_kernel(place, info, emb_info, q, e, total, _, turned):
    match = matching(place)
    columns = place[2] + lax.broadcasted_iota(jnp.int32, (SLAB, turned.shape[0]), 1)
    for d in range(4):
        part = pl.ds(d * SLAB, SLAB)
        tot = as_column(match, total[d : d + 1, :])
        hits = (columns == joined(info[part, :])).astype(F32)
        weight = info[part, 3:4].astype(F32)
        s = q[part, :]
        value = (weight * (e[part, :] / tot - hits) * (1.0 - s * s)).astype(BF16)
        turned[:, d * SLAB : (d + 1) * SLAB] = value.T
        hit = (columns == joined(emb_info[part, :])).astype(F32).astype(BF16)
        turned[:, (4 + d) * SLAB : (5 + d) * SLAB] = hit.T


def dlogit_call(place, hid, emb, q, e, total, after):
    (tokens, rows), half = q.shape, hid.shape[1] - INFO
    every = lambda a: pl.BlockSpec(a.shape, lambda i, p: (0, 0))
    return pl.pallas_call(
        dlogit_kernel,
        grid_spec=pltpu.PrefetchScalarGridSpec(
            num_scalar_prefetch=1,
            grid=(1,),
            in_specs=[pl.BlockSpec((tokens, INFO), lambda i, p: (0, half // INFO))] * 2
            + [every(a) for a in (q, e, total)]
            + [pl.BlockSpec(memory_space=pl.ANY)],
            out_specs=pl.BlockSpec((rows, 2 * tokens), lambda i, p: (0, 0)),
        ),
        out_shape=jax.ShapeDtypeStruct((rows, 2 * tokens), BF16),
        compiler_params=params(),
        cost_estimate=cost(0),
        name="dlogit",
    )(place, hid, emb, q, e, total, after)


def table_grad_kernel(place, turned, hid, emb, *refs):
    out, tokens = refs[-1], hid.shape[0]
    acc = jnp.dot(turned[:, :tokens], hid[...], preferred_element_type=F32)
    acc += jnp.dot(turned[:, tokens:], emb[...], preferred_element_type=F32)
    out[...] = acc.astype(BF16)


def table_grad_call(place, turned, hid, emb, other, before=None):
    rows, (tokens, width) = turned.shape[0], hid.shape
    half = width - INFO
    steps = half // TILE
    return pl.pallas_call(
        table_grad_kernel,
        grid_spec=pltpu.PrefetchScalarGridSpec(
            num_scalar_prefetch=1,
            grid=(steps,),
            in_specs=[pl.BlockSpec(turned.shape, lambda j, p: (0, 0))]
            + [pl.BlockSpec((tokens, TILE), lambda j, p: (0, j))] * 2
            + ([] if before is None else [pl.BlockSpec(memory_space=pl.ANY)]),
            out_specs=pl.BlockSpec(
                (rows, TILE),
                lambda j, p: (0, (1 - p[0] if other else p[0]) * steps + j),
            ),
        ),
        out_shape=jax.ShapeDtypeStruct((rows, 2 * half), BF16),
        input_output_aliases={} if before is None else {4: 0},
        compiler_params=params(),
        cost_estimate=cost(0),
        name="table_grad",
    )(place, turned, hid, emb, *([] if before is None else [before]))


def spread(value, axes, size=16):
    return lax.all_to_all(jnp.broadcast_to(value, (size,) + value.shape), axes, 0, 0)


def body(hidden, table, target_ids, loss_weight, input_ids, emb_grad_in):
    own_rows, width = table.shape
    half = width // 2
    core = lax.axis_index("c")
    row_start = lax.axis_index(AXES) * own_rows
    place = jnp.stack(
        [core, lax.axis_index("zh"), row_start, row_start + (1 - 2 * core) * own_rows]
    ).astype(jnp.int32)

    def my_half(a):
        return lax.dynamic_slice_in_dim(a, core * half, half, 1)

    joint = jnp.concatenate(
        [
            my_half(hidden),
            info_columns(digits(target_ids) + [loss_weight]),
            my_half(emb_grad_in),
            info_columns(digits(input_ids)),
        ],
        1,
    )
    joint = jnp.concatenate([joint] + [pull(joint, "zh", d) for d in (1, 2, 3)], 0)
    t_send = lax.dynamic_slice_in_dim(table, (1 - core) * half, half, 1)
    hid = joint[:, : half + INFO] + t_send[:1, :1] * 0
    hid = spread(hid, ("x", "y")).reshape(4 * SLAB, half + INFO)
    emb = joint[:, half + INFO :]
    emb = jnp.concatenate([emb] + [pull(emb, "y", d) for d in (1, 2, 3)], 0)
    t_other = swap(t_send, "c")

    hid_other = swap(hid, "c")
    q, e, slope, sums, gate = logits_call(place, hid, hid_other, table, emb)
    emb = emb + gate.astype(BF16)
    columns = [pull(emb, "x", d) for d in (1, 2, 3)]
    tokens, rows = slope.shape
    full = pl.BlockSpec((tokens, rows), lambda j, p: (0, 0))
    mean, _ = product_call(
        mean_kernel, place, [slope, swap(slope, "c")], [full, full], table, t_other, F32, [], "mean"
    )
    each = jnp.broadcast_to(sums, (16,) + sums.shape)
    total, gate = total_call(each, ("zh", "zl", "c"), mean, each.shape)
    pick, gate = product_call(
        pick_kernel,
        place,
        [hid, mean],
        [
            pl.BlockSpec((tokens, INFO), lambda j, p: (0, half // INFO)),
            pl.BlockSpec(memory_space=pl.ANY),
        ],
        table,
        t_other,
        BF16,
        [pltpu.VMEM((tokens, rows), BF16)] * 2,
        "pick",
    )
    emb = jnp.concatenate([emb + gate.astype(BF16)] + columns, 0)
    emb_other = swap(emb, "c")
    total, _ = total_call(total, ("x", "y"), pick, sums.shape)

    out = combine_call(place, hid, mean, pick, total)
    got = lax.all_to_all(out.reshape(16, 32, half), ("x", "y"), 0, 0)

    turned = dlogit_call(place, hid, emb, q, e, total, out)
    grad_table = table_grad_call(place, turned, hid, emb, 0)
    grad_table = table_grad_call(place, turned, hid_other, emb_other, 1, grad_table)

    acc = sum_call(got, grad_table)
    acc = lax.dynamic_slice_in_dim(
        jnp.concatenate([acc, acc], 0), (4 - lax.axis_index("zh")) % 4 * 8, 32, 0
    )
    acc = jnp.broadcast_to(acc.reshape(4, 1, 8, half), (4, 2, 8, half)).reshape(8, 8, half)
    acc = lax.all_to_all(acc, ("zh", "zl"), 0, 0)
    acc = jnp.sum(acc.astype(F32), 0).astype(BF16)
    grad_hidden = whole(core, acc, swap(acc, "c"))
    return grad_hidden, grad_table


def solution(mesh):
    fine = Mesh(mesh.devices.reshape(4, 4, 4, 2, 2), AXES)
    rows, every = P(DP, None), P(AXES, None)
    return jax.shard_map(
        body,
        mesh=fine,
        in_specs=(rows, every, P(DP), P(DP), P(DP), rows),
        out_specs=(rows, every),
        check_vma=False,
    )
```
